256 devices in a mesh: grp: 8 (over y, x_lo), afd: 32 (over x_hi, z, core).
Axes of the slice: x: 4 (x_hi: 2, x_lo: 2; x = x_hi * 2 + x_lo), y: 4, z: 8, core: 2. Of those that a mesh axis runs over, the one named last changes fastest.
Arguments:
- queries: bfloat16 [4096, 8192], P(('grp', 'afd')), parts along dimension 0, may hold values from -500 to 500
- key_cache: bfloat16 [4096, 128, 256], P(('grp', 'afd')), parts along dimension 0, may hold values from -4.05 to 4.05
- value_cache: bfloat16 [4096, 128, 256], P(('grp', 'afd')), parts along dimension 0, may hold values from -4 to 4
- lengths: int32 [4096], P(('grp', 'afd')), parts along dimension 0, may hold values from 2 to 128, as said below
- out_proj: bfloat16 [8192, 7168], P('afd'), may hold values from -0.375 to 0.375
- residual: bfloat16 [4096, 7168], P(('grp', 'afd')), parts along dimension 0, may hold values from -6 to 6
- routes: int32 [4096, 3], P(('grp', 'afd')), parts along dimension 0, may hold values from 0 to 47, as said below
- route_weight: float32 [4096, 3], P(('grp', 'afd')), parts along dimension 0, may hold values from 0.25 to 1
- w_gate: bfloat16 [5120, 7168], P('afd'), may hold values from -0.0625 to 0.0625
- w_up: bfloat16 [5120, 7168], P('afd'), may hold values from -0.0625 to 0.0625
- w_down: bfloat16 [5120, 7168], P('afd'), may hold values from -0.078125 to 0.078125
Outputs:
- layer_out: bfloat16 [4096, 7168], P(('grp', 'afd')), parts along dimension 0
The draws below stay inside these ranges and needn't reach their ends.
There are 8 independent parts, one for each index of `grp`. The reference program is written for one: setup_inputs(seed, part) draws one part's arguments, and reference() takes and returns one part's arrays. A program takes and returns all parts, laid end to end along the dimension named above; an argument that names none is the same for every part. Nothing has to cross between parts.
Inputs may be any that keep to these rules, and one draw needn't show every extreme that they name: `routes`: each row names 3 different experts. Within the 16 rows of one device, expert 0 is named by 1 to 8 rows, and by exactly 8 rows on some device. `lengths`: some request has all 128 positions valid.
All inputs are finite; a program needn't handle non-finite values.
Results may differ from the reference program's by a relative error of at most 0.02.
Values may be sent and summed in bfloat16 or wider, within the bound.
No kernel may reach another device: no remote copies, remote signals or barrier semaphores. Data moves between devices by JAX's collectives and lax.ppermute only.
A program may use at most 128 MiB of HBM per device.

```python
import math
import jax
import jax.numpy as jnp
from jax import lax

D = 7168
HQ = 32
HS = 256
FF = 5120
EXPERTS = 48
TOPK = 3
REQ_DEV = 16
LMAX = 128
CAP = 8
REQUESTS = 512
N_AFD = 32


def cache_keys(key):
    return jnp.clip(jax.random.normal(key, (REQUESTS, LMAX, HS), jnp.float32), -4.0, 4.0)


def draw_key_cache(key, part):
    shared = cache_keys(key)
    return shared.astype(jnp.bfloat16)


def draw_queries(key, part):
    key = jax.random.fold_in(key, 3)
    drawn = jnp.clip(jax.random.normal(key, (REQUESTS, HQ * HS), jnp.float32), -4.0, 4.0)
    return drawn.astype(jnp.bfloat16)


def draw_lengths(key, part):
    key = jax.random.fold_in(key, 7)
    first, second = jax.random.split(key)
    spans = jax.random.randint(first, (REQUESTS,), 2, LMAX + 1)
    place = jax.random.randint(second, (), 0, REQUESTS)
    return jnp.where(jnp.arange(REQUESTS) == place, LMAX, spans).astype(jnp.int32)


def draw_routes(key, part):
    key = jax.random.fold_in(key, 5)
    keys = jax.random.split(key, 5)
    devices = REQUESTS // REQ_DEV
    counts = jax.random.randint(keys[0], (devices,), 1, CAP + 1)
    busiest = jax.random.randint(keys[1], (), 0, devices)
    counts = jnp.where(jnp.arange(devices) == busiest, CAP, counts)
    priority = jax.random.randint(keys[2], (devices, REQ_DEV), 0, 65536) * REQ_DEV + jnp.arange(REQ_DEV)[None, :]
    ranking = jnp.argsort(jnp.argsort(priority, axis=1), axis=1)
    chosen = (ranking < counts[:, None]).reshape(REQUESTS)
    scores = jax.random.randint(keys[3], (REQUESTS, EXPERTS - 1), 0, 65536) * EXPERTS + jnp.arange(EXPERTS - 1)[None, :]
    others = lax.top_k(scores, TOPK)[1] + 1
    position = jax.random.randint(keys[4], (REQUESTS,), 0, TOPK)
    placed = chosen[:, None] & (jnp.arange(TOPK)[None, :] == position[:, None])
    return jnp.where(placed, 0, others).astype(jnp.int32)


def block_scale(stream_key, shape, cuts, least, top_value):
    def one(axis_at, parts):
        heights = jax.random.uniform(jax.random.fold_in(jax.random.fold_in(stream_key, 6), axis_at), (parts,), jnp.float32, least / len(cuts), top_value / len(cuts))
        return jnp.repeat(jnp.exp(heights), shape[axis_at] // parts).reshape((-1,) + (1,) * (len(shape) - axis_at - 1))

    gain = one(*cuts[0])
    for cut in cuts[1:]:
        gain = gain * one(*cut)
    return gain


def scatter_about(own_key, extent, deviation, reach, pieces=(), kind=jnp.bfloat16):
    array = jax.random.normal(own_key, extent, jnp.float32) * deviation
    if len(pieces) > 0:
        array = block_scale(own_key, extent, pieces, -0.22, 0.18) * array
    return jnp.clip(array, min=-reach, max=reach).astype(kind)


def setup_inputs(seed: int = 0, part: int = 0) -> dict:
    arg_keys = jax.random.split(jax.random.key(seed), 12)
    part_splits = jax.random.split(jax.random.fold_in(arg_keys[11], part), 12)
    queries = draw_queries(jax.random.fold_in(jax.random.fold_in(arg_keys[11], part), 71), part)
    key_cache = draw_key_cache(jax.random.fold_in(jax.random.fold_in(arg_keys[11], part), 71), part)
    value_cache = scatter_about(part_splits[2], (REQUESTS, LMAX, HS), 1.0, 4.0, ((0, 32),))
    lengths = draw_lengths(jax.random.fold_in(jax.random.fold_in(arg_keys[11], part), 71), part)
    out_proj = scatter_about(arg_keys[4], (HQ * HS, D), HS ** -0.5, 0.375, ((0, 32),))
    residual = scatter_about(part_splits[5], (REQUESTS, D), 1.0, 6.0, ((0, 32),))
    routes = draw_routes(jax.random.fold_in(jax.random.fold_in(arg_keys[11], part), 71), part)
    route_weight = jnp.clip(jnp.exp(math.log(1.0) - 1.3862944 * jax.random.uniform(part_splits[7], (REQUESTS, TOPK), jnp.float32) ** block_scale(part_splits[7], (REQUESTS, TOPK), ((0, 32),), -0.2, 0.2)), 0.25, 1.0)
    w_gate = scatter_about(arg_keys[8], (FF, D), D ** -0.5, 0.0625, ((0, 32),))
    w_up = scatter_about(arg_keys[9], (FF, D), D ** -0.5, 0.0625, ((0, 32),))
    w_down = scatter_about(arg_keys[10], (FF, D), FF ** -0.5, 0.078125, ((0, 32),))
    return dict(queries=queries, key_cache=key_cache, value_cache=value_cache, lengths=lengths, out_proj=out_proj, residual=residual, routes=routes, route_weight=route_weight, w_gate=w_gate, w_up=w_up, w_down=w_down)


def attend(queries, key_cache, value_cache, lengths):
    count_rows = queries.shape[0]
    grouped = queries.reshape(count_rows, HQ, HS).astype(jnp.float32)
    scores = jnp.einsum('rhd,rld->rhl', grouped, key_cache.astype(jnp.float32)) / math.sqrt(HS)
    positions = lax.broadcasted_iota(jnp.int32, (1, 1, LMAX), 2)
    scores = jnp.where(positions < lengths.astype(jnp.int32)[:, None, None], scores, -1e+30)
    largest = lax.optimization_barrier(jnp.max(scores, axis=2, keepdims=True))
    expo = jnp.exp(scores - largest)
    weights = (expo / lax.optimization_barrier(jnp.sum(expo, axis=2, keepdims=True))).astype(jnp.bfloat16)
    mixed = jnp.einsum('rhl,rld->rhd', weights.astype(jnp.float32), value_cache.astype(jnp.float32))
    return mixed.astype(jnp.bfloat16).reshape(count_rows, HQ * HS)

def reference(queries, key_cache, value_cache, lengths, out_proj, residual, routes, route_weight, w_gate, w_up, w_down):
    attended = attend(queries, key_cache, value_cache, lengths)
    width_slice = HQ * HS // N_AFD
    blocks = attended.reshape(REQUESTS, N_AFD, width_slice).transpose(1, 0, 2)
    weight_blocks = out_proj.reshape(N_AFD, width_slice, D)

    def add_block(total, pair):
        block, weights = pair
        term = jnp.dot(block, weights, preferred_element_type=jnp.float32).astype(jnp.bfloat16)
        term = lax.optimization_barrier(term)
        return (total + term.astype(jnp.float32), None)
    projected, unused = lax.scan(add_block, jnp.zeros((REQUESTS, D), jnp.float32), (blocks, weight_blocks))
    hidden_state = residual.astype(jnp.float32) + projected
    normed = (hidden_state * lax.rsqrt(lax.optimization_barrier(jnp.mean(hidden_state * hidden_state, axis=1, keepdims=True)) + 1e-06)).astype(jnp.bfloat16)
    expert_share = lax.optimization_barrier(jnp.sum(jnp.where(routes == 0, route_weight, 0.0), axis=1))
    gate_part = jnp.dot(normed, w_gate.T, preferred_element_type=jnp.float32)
    up_part = jnp.dot(normed, w_up.T, preferred_element_type=jnp.float32)
    activated = (jax.nn.silu(gate_part) * up_part).astype(jnp.bfloat16)
    expert_rows = jnp.dot(activated, w_down, preferred_element_type=jnp.float32)
    return (hidden_state + expert_share[:, None] * expert_rows).astype(jnp.bfloat16)
```

```python
import functools
import math

import jax
import jax.numpy as jnp
from jax import lax
from jax.experimental import pallas as pl
from jax.experimental.pallas import tpu as pltpu
from jax.sharding import Mesh
from jax.sharding import PartitionSpec as P

D = 7168
HS = 256
CAP = 8
NX = 2
NZ = 8
CHIPS = NX * NZ
ROWS = 16
AXES = ("y", "xlo", "xhi", "z", "core")
RING = ("xhi", "z")
CUT = 3584


def attend(queries, key_cache, value_cache, lengths):
    count_rows = queries.shape[0]
    cache_len = key_cache.shape[1]
    head_size = key_cache.shape[2]
    num_heads = queries.shape[1] // head_size
    grouped = queries.reshape(count_rows, num_heads, head_size)
    scores = jnp.einsum(
        "rhd,rld->rhl", grouped, key_cache, preferred_element_type=jnp.float32
    ) / math.sqrt(head_size)
    positions = lax.broadcasted_iota(jnp.int32, (1, 1, cache_len), 2)
    scores = jnp.where(positions < lengths[:, None, None], scores, -1e30)
    largest = jnp.max(scores, axis=2, keepdims=True)
    expo = jnp.exp(scores - largest)
    weights = (expo / jnp.sum(expo, axis=2, keepdims=True)).astype(jnp.bfloat16)
    mixed = jnp.einsum("rhl,rld->rhd", weights, value_cache, preferred_element_type=jnp.float32)
    return mixed.astype(jnp.bfloat16).reshape(count_rows, num_heads * head_size)


def swap_cores(a):
    return lax.ppermute(a, "core", [(0, 1), (1, 0)])


def swap_x(a):
    return lax.ppermute(a, "xhi", [(0, 1), (1, 0)])


def shift(a, by):
    return lax.ppermute(a, "z", [(i, (i + by) % NZ) for i in range(NZ)])


def add(*terms):
    total = terms[0].astype(jnp.float32)
    for term in terms[1:]:
        total = total + term.astype(jnp.float32)
    return total


def add16(*terms):
    return add(*terms).astype(jnp.bfloat16)


def sum_z(part):
    half = part[0].shape[-1] // 2
    up = shift(part[4][..., :half], 1)
    down = shift(part[4][..., half:], -1)
    up = shift(jnp.concatenate([add16(part[3][..., :half], up), part[3][..., half:]], axis=-1), 1)
    down = shift(jnp.concatenate([part[5][..., :half], add16(part[5][..., half:], down)], axis=-1), -1)
    up = shift(add16(part[2], up), 1)
    down = shift(add16(part[6], down), -1)
    up = shift(add16(part[1], up), 1)
    down = shift(add16(part[7], down), -1)
    return part[0], up, down


def sum_x_first(part):
    other = swap_x(part[1])
    mine = add16(part[0], other)
    return add(*sum_z([mine[k] for k in range(NZ)]))


def sum_z_first(part):
    got = add16(*sum_z([part[:, k] for k in range(NZ)]))
    return add(got[0], swap_x(got[1]))


def scatter_sum(part):
    return jnp.concatenate(
        [sum_x_first(part[..., :CUT]), sum_z_first(part[..., CUT:])], axis=-1
    )


def gather_z(mine):
    half = mine.shape[-1] // 2
    a1, b1 = shift(mine, 1), shift(mine, -1)
    a2, b2 = shift(a1, 1), shift(b1, -1)
    a3, b3 = shift(a2, 1), shift(b2, -1)
    a4, b4 = shift(a3[..., :half], 1), shift(b3[..., half:], -1)
    return [mine, b1, b2, b3, jnp.concatenate([a4, b4], axis=-1), a3, a2, a1]


def gather(mine):
    near = jnp.stack(gather_z(mine[:, :CUT]))
    first = jnp.stack([near, swap_x(near)])
    pair = jnp.stack([mine[:, CUT:], swap_x(mine[:, CUT:])])
    second = jnp.stack(gather_z(pair), axis=1)
    return jnp.concatenate([first, second], axis=-1)


def project_kernel(place, a_own, a_oth, w_own, w_oth, out, own, oth):
    @pl.when(pl.program_id(0) == 0)
    def _():
        for rx in range(NX):
            for rz in range(NZ):
                x = lax.rem(place[0] + rx, NX)
                z = lax.rem(place[1] + rz, NZ)
                at = pl.multiple_of((x * NZ + z) * ROWS, ROWS)
                to = pl.ds((rx * NZ + rz) * ROWS, ROWS)
                own[to, :] = a_own[pl.ds(at, ROWS), :]
                oth[to, :] = a_oth[pl.ds(at, ROWS), :]

    total = jnp.dot(own[...], w_own[...], preferred_element_type=jnp.float32)
    total += jnp.dot(oth[...], w_oth[...], preferred_element_type=jnp.float32)
    out[...] = total.astype(jnp.bfloat16)


def project(place, attended, w_own, w_oth, tile=1024):
    rows, depth = attended.shape[0], w_own.shape[0]
    return pl.pallas_call(
        project_kernel,
        out_shape=jax.ShapeDtypeStruct((rows, D), jnp.bfloat16),
        grid_spec=pltpu.PrefetchScalarGridSpec(
            num_scalar_prefetch=1,
            grid=(D // tile,),
            in_specs=[
                pl.BlockSpec((rows, depth), lambda i, s: (0, s[2])),
                pl.BlockSpec((rows, depth), lambda i, s: (0, 1 - s[2])),
                pl.BlockSpec((depth, tile), lambda i, s: (0, i)),
                pl.BlockSpec((depth, tile), lambda i, s: (0, i)),
            ],
            out_specs=pl.BlockSpec((rows, tile), lambda i, s: (0, i)),
            scratch_shapes=[
                pltpu.VMEM((rows, depth), jnp.bfloat16),
                pltpu.VMEM((rows, depth), jnp.bfloat16),
            ],
        ),
        compiler_params=pltpu.CompilerParams(vmem_limit_bytes=32 * 1024 * 1024),
        name="project",
    )(place, attended, attended, w_own, w_oth)


def expert_kernel(steps, rows_in, g_own, g_oth, u_own, u_oth, d_own, d_oth, out, gate, up, act):
    i = pl.program_id(0)
    dims = (((1,), (1,)), ((), ()))

    @pl.when(i == 0)
    def _():
        gate[...] = jnp.zeros_like(gate)
        up[...] = jnp.zeros_like(up)

    @pl.when(i < steps)
    def _():
        piece = rows_in[...]
        g = jnp.concatenate([g_own[...], g_oth[...]], axis=0)
        u = jnp.concatenate([u_own[...], u_oth[...]], axis=0)
        gate[...] += lax.dot_general(piece, g, dims, preferred_element_type=jnp.float32)
        up[...] += lax.dot_general(piece, u, dims, preferred_element_type=jnp.float32)

    @pl.when(i == steps - 1)
    def _():
        g = gate[...]
        act[...] = (g / (1.0 + jnp.exp(-g)) * up[...]).astype(jnp.bfloat16)

    @pl.when(i >= steps)
    def _():
        d = jnp.concatenate([d_own[...], d_oth[...]], axis=0)
        out[...] = jnp.dot(act[...], d, preferred_element_type=jnp.float32).astype(jnp.bfloat16)


def expert(rows_in, g_own, g_oth, u_own, u_oth, d_own, d_oth, tile=1024):
    rows, units = rows_in.shape[0], g_own.shape[0]
    steps = D // tile
    first = pl.BlockSpec((units, tile), lambda i: (0, jnp.minimum(i, steps - 1)))
    last = pl.BlockSpec((units, tile), lambda i: (0, jnp.maximum(i - steps, 0)))
    return pl.pallas_call(
        functools.partial(expert_kernel, steps),
        out_shape=jax.ShapeDtypeStruct((rows, D), jnp.bfloat16),
        grid=(2 * steps,),
        in_specs=[
            pl.BlockSpec((rows, tile), lambda i: (0, jnp.minimum(i, steps - 1))),
            first,
            first,
            first,
            first,
            last,
            last,
        ],
        out_specs=pl.BlockSpec((rows, tile), lambda i: (0, jnp.maximum(i - steps, 0))),
        scratch_shapes=[
            pltpu.VMEM((rows, 2 * units), jnp.float32),
            pltpu.VMEM((rows, 2 * units), jnp.float32),
            pltpu.VMEM((rows, 2 * units), jnp.bfloat16),
        ],
        compiler_params=pltpu.CompilerParams(vmem_limit_bytes=32 * 1024 * 1024),
        name="expert",
    )(rows_in, g_own, g_oth, u_own, u_oth, d_own, d_oth)


def slots(routes):
    named = jnp.any(routes == 0, axis=1)
    row = jnp.arange(ROWS)
    before = row[:, None] < row[None, :]
    n_named = jnp.sum(named)
    rank_named = jnp.sum((before & named[:, None]).astype(jnp.int32), axis=0)
    slot = jnp.where(named, rank_named, n_named + row - rank_named)
    return row[:, None] == slot[None, :]


def body(
    queries,
    key_cache,
    value_cache,
    lengths,
    out_proj,
    residual,
    routes,
    route_weight,
    w_gate,
    w_up,
    w_down,
):
    place = jnp.stack([lax.axis_index(a) for a in ("xhi", "z", "core")]).astype(jnp.int32)
    o_oth = swap_cores(out_proj)
    g_oth, u_oth, d_oth = swap_cores(w_gate), swap_cores(w_up), swap_cores(w_down)

    order = slots(routes)
    order16 = order.astype(jnp.bfloat16)
    share = jnp.sum(jnp.where(routes == 0, route_weight, 0.0), axis=1)
    share = jnp.sum(jnp.where(order, share[None, :], 0.0), axis=1)

    attended = attend(queries, key_cache, value_cache, lengths)
    attended = jnp.dot(order16, attended, preferred_element_type=jnp.float32).astype(jnp.bfloat16)
    by_heads = lax.all_to_all(attended, RING, split_axis=1, concat_axis=0, tiled=True)
    parts = project(place, by_heads, out_proj, o_oth).reshape(NX, NZ, ROWS, D)
    res = jnp.dot(order16, residual, preferred_element_type=jnp.float32)
    hidden_state = res + scatter_sum(parts)
    chosen = hidden_state[:CAP]
    normed = (
        chosen * lax.rsqrt(jnp.mean(chosen * chosen, axis=1, keepdims=True) + 1e-06)
    ).astype(jnp.bfloat16)
    everyone = gather(normed).reshape(CHIPS * CAP, D)
    rows = expert(everyone, w_gate, g_oth, w_up, u_oth, w_down, d_oth)
    expert_rows = scatter_sum(rows.reshape(NX, NZ, CAP, D))
    done = jnp.concatenate(
        [chosen + share[:CAP, None] * expert_rows, hidden_state[CAP:] + share[CAP:, None] * 0.0], axis=0
    ).astype(jnp.bfloat16)
    return jnp.dot(order16.T, done, preferred_element_type=jnp.float32).astype(jnp.bfloat16)


def solution(mesh):
    fine = Mesh(mesh.devices.reshape(4, 2, NX, NZ, 2), AXES)
    rows, weights = P(AXES, None), P(("xhi", "z", "core"), None)
    placed = (
        rows,
        P(AXES, None, None),
        P(AXES, None, None),
        P(AXES),
        weights,
        rows,
        rows,
        rows,
        weights,
        weights,
        weights,
    )
    return jax.shard_map(body, mesh=fine, in_specs=placed, out_specs=rows, check_vma=False)
```

```python
import functools
import math

import jax
import jax.numpy as jnp
from jax import lax
from jax.experimental import pallas as pl
from jax.experimental.pallas import tpu as pltpu
from jax.sharding import Mesh
from jax.sharding import PartitionSpec as P

D = 7168
HS = 256
CAP = 8
NX = 2
NZ = 8
CHIPS = NX * NZ
ROWS = 16
AXES = ("y", "xlo", "xhi", "z", "core")
RING = ("xhi", "z")
VMEM_LIMIT = 16 * 1024 * 1024


def attend(queries, key_cache, value_cache, lengths):
    count_rows = queries.shape[0]
    cache_len = key_cache.shape[1]
    head_size = key_cache.shape[2]
    num_heads = queries.shape[1] // head_size
    grouped = queries.reshape(count_rows, num_heads, head_size)
    scores = jnp.einsum(
        "rhd,rld->rhl", grouped, key_cache, preferred_element_type=jnp.float32
    ) / math.sqrt(head_size)
    positions = lax.broadcasted_iota(jnp.int32, (1, 1, cache_len), 2)
    scores = jnp.where(positions < lengths[:, None, None], scores, -1e30)
    largest = jnp.max(scores, axis=2, keepdims=True)
    expo = jnp.exp(scores - largest)
    weights = (expo / jnp.sum(expo, axis=2, keepdims=True)).astype(jnp.bfloat16)
    mixed = jnp.einsum("rhl,rld->rhd", weights, value_cache, preferred_element_type=jnp.float32)
    return mixed.astype(jnp.bfloat16).reshape(count_rows, num_heads * head_size)


def swap_cores(a):
    return lax.ppermute(a, "core", [(0, 1), (1, 0)])


def swap_x(a):
    return lax.ppermute(a, "xhi", [(0, 1), (1, 0)])


def shift(a, by):
    return lax.ppermute(a, "z", [(i, (i + by) % NZ) for i in range(NZ)])


def add(*terms):
    total = terms[0].astype(jnp.float32)
    for term in terms[1:]:
        total = total + term.astype(jnp.float32)
    return total


def add16(*terms):
    return add(*terms).astype(jnp.bfloat16)


def sum_z(part):
    half = part[0].shape[-1] // 2
    up, down = shift(part[3], 1), shift(part[5], -1)
    far_up, far_down = shift(part[4][..., :half], 2), shift(part[4][..., half:], -2)
    up = shift(add_part(part[2], up, far_up, 0), 1)
    down = shift(add_part(part[6], down, far_down, half), -1)
    up = shift(add16(part[1], up), 1)
    down = shift(add16(part[7], down), -1)
    return part[0], up, down


def add_part(whole, other, piece, at):
    size = piece.shape[-1]
    rest = whole.shape[-1] - size - at
    piece = jnp.pad(piece, ((0, 0), (at, rest)))
    return add16(whole, other, piece)


def sum_z_x(part):
    rows = part.shape[0] // CHIPS
    both = NX * rows
    got = add16(*sum_z([part[k * both : (k + 1) * both] for k in range(NZ)]))
    return add(got[:rows], swap_x(got[rows:]))


def gather_z(mine):
    half = mine.shape[-1] // 2
    a1, b1 = shift(mine, 1), shift(mine, -1)
    a2, b2 = shift(a1, 1), shift(b1, -1)
    a3, b3 = shift(a2, 1), shift(b2, -1)
    a4, b4 = shift(a3[..., :half], 1), shift(b3[..., half:], -1)
    return [mine, b1, b2, b3, a4, b4, a3, a2, a1]


def project_kernel(tile, place, a_own, a_oth, w_own, w_oth, out, own, oth):
    for rz in range(NZ):
        for rx in range(NX):
            x = lax.rem(place[0] + rx, NX)
            z = lax.rem(place[1] + rz, NZ)
            chip = x * NZ + z
            own[rz * NX + rx] = a_own[chip].astype(jnp.float32)
            oth[rz * NX + rx] = a_oth[chip].astype(jnp.float32)
    rows = out.shape[0]
    first = own[...].reshape(rows, own.shape[2]).astype(jnp.bfloat16)
    second = oth[...].reshape(rows, oth.shape[2]).astype(jnp.bfloat16)

    @pl.loop(0, D // tile)
    def _(i):
        at = pl.ds(pl.multiple_of(i * tile, tile), tile)
        total = jnp.dot(first, w_own[:, at], preferred_element_type=jnp.float32)
        total += jnp.dot(second, w_oth[:, at], preferred_element_type=jnp.float32)
        out[:, at] = total.astype(jnp.bfloat16)


def project(place, attended, w_own, w_oth, tile=512):
    chips, count, _ = attended.shape
    depth = w_own.shape[0]
    whole = pl.BlockSpec(memory_space=pltpu.VMEM)
    return pl.pallas_call(
        functools.partial(project_kernel, tile),
        out_shape=jax.ShapeDtypeStruct((chips * count, D), jnp.bfloat16),
        grid_spec=pltpu.PrefetchScalarGridSpec(
            num_scalar_prefetch=1,
            grid=(1,),
            in_specs=[
                pl.BlockSpec((chips, count, depth), lambda i, s: (0, 0, s[2])),
                pl.BlockSpec((chips, count, depth), lambda i, s: (0, 0, 1 - s[2])),
                whole,
                whole,
            ],
            out_specs=whole,
            scratch_shapes=[
                pltpu.VMEM((chips, count, depth), jnp.float32),
                pltpu.VMEM((chips, count, depth), jnp.float32),
            ],
        ),
        compiler_params=pltpu.CompilerParams(vmem_limit_bytes=VMEM_LIMIT),
        name="project",
    )(place, attended, attended, w_own, w_oth)


def expert_kernel(tile, *refs):
    pieces, (g_own, g_oth, u_own, u_oth, d_own, d_oth, out) = refs[:9], refs[9:]
    steps, units = D // tile, g_own.shape[0]
    dims = (((1,), (1,)), ((), ()))
    rows = out.shape[0]
    gate = jnp.zeros((rows, 2 * units), jnp.float32)
    up = jnp.zeros((rows, 2 * units), jnp.float32)
    for i in range(steps):
        at = slice(i * tile, (i + 1) * tile)
        if i < steps // 2:
            far = pieces[4][:, at]
        else:
            far = pieces[5][:, i * tile - D // 2 : (i + 1) * tile - D // 2]
        near = [p[:, at] for p in pieces[:4]]
        back = [p[:, at] for p in pieces[6:]]
        piece = jnp.concatenate(near + [far] + back, axis=0)
        g = jnp.concatenate([g_own[:, at], g_oth[:, at]], axis=0)
        u = jnp.concatenate([u_own[:, at], u_oth[:, at]], axis=0)
        gate += lax.dot_general(piece, g, dims, preferred_element_type=jnp.float32)
        up += lax.dot_general(piece, u, dims, preferred_element_type=jnp.float32)
    act = (gate / (1.0 + jnp.exp(-gate)) * up).astype(jnp.bfloat16)

    @pl.loop(0, steps)
    def _(i):
        at = pl.ds(pl.multiple_of(i * tile, tile), tile)
        d = jnp.concatenate([d_own[:, at], d_oth[:, at]], axis=0)
        out[:, at] = jnp.dot(act, d, preferred_element_type=jnp.float32).astype(jnp.bfloat16)


def expert(pieces, weights, tile=896):
    whole = pl.BlockSpec(memory_space=pltpu.VMEM)
    return pl.pallas_call(
        functools.partial(expert_kernel, tile),
        out_shape=jax.ShapeDtypeStruct((CHIPS * CAP, D), jnp.bfloat16),
        in_specs=[whole] * (len(pieces) + len(weights)),
        out_specs=whole,
        compiler_params=pltpu.CompilerParams(vmem_limit_bytes=VMEM_LIMIT),
        name="expert",
    )(*pieces, *weights)


def slots(routes):
    named = jnp.any(routes == 0, axis=1)
    row = jnp.arange(ROWS)
    before = row[:, None] < row[None, :]
    n_named = jnp.sum(named)
    rank_named = jnp.sum((before & named[:, None]).astype(jnp.int32), axis=0)
    slot = jnp.where(named, rank_named, n_named + row - rank_named)
    return row[:, None] == slot[None, :]


def body(
    queries,
    key_cache,
    value_cache,
    lengths,
    out_proj,
    residual,
    routes,
    route_weight,
    w_gate,
    w_up,
    w_down,
):
    place = jnp.stack([lax.axis_index(a) for a in ("xhi", "z", "core")]).astype(jnp.int32)
    o_oth = swap_cores(out_proj)
    g_oth, u_oth, d_oth = swap_cores(w_gate), swap_cores(w_up), swap_cores(w_down)

    order = slots(routes)
    order16 = order.astype(jnp.bfloat16)
    share = jnp.sum(jnp.where(routes == 0, route_weight, 0.0), axis=1)
    share = jnp.sum(jnp.where(order, share[None, :], 0.0), axis=1)

    attended = attend(queries, key_cache, value_cache, lengths)
    attended = jnp.dot(order16, attended, preferred_element_type=jnp.float32).astype(jnp.bfloat16)
    by_heads = lax.all_to_all(
        attended.reshape(2, CAP, CHIPS, 2 * HS), RING, split_axis=2, concat_axis=1
    )
    by_heads, o_oth, g_oth, u_oth, d_oth = lax.optimization_barrier(
        (by_heads, o_oth, g_oth, u_oth, d_oth)
    )
    res = jnp.dot(order16, residual, preferred_element_type=jnp.float32)

    chosen_part = project(place, by_heads[0], out_proj, o_oth)
    fixed = place * jnp.array([1, 0, 1], jnp.int32)
    other_part = project(fixed, by_heads[1], out_proj, o_oth)
    other_part = lax.psum_scatter(other_part, "z", scatter_dimension=0, tiled=True)

    chosen = res[:CAP] + sum_z_x(chosen_part)
    normed = (
        chosen * lax.rsqrt(jnp.mean(chosen * chosen, axis=1, keepdims=True) + 1e-06)
    ).astype(jnp.bfloat16)
    pieces = gather_z(jnp.concatenate([normed, swap_x(normed)], axis=0))
    rows = expert(pieces, (w_gate, g_oth, w_up, u_oth, w_down, d_oth))
    expert_rows = sum_z_x(rows)
    others = res[CAP:] + add(other_part[:CAP], swap_x(other_part[CAP:]))
    done = jnp.concatenate(
        [chosen + share[:CAP, None] * expert_rows, others], axis=0
    ).astype(jnp.bfloat16)
    return jnp.dot(order16.T, done, preferred_element_type=jnp.float32).astype(jnp.bfloat16)


def solution(mesh):
    fine = Mesh(mesh.devices.reshape(4, 2, NX, NZ, 2), AXES)
    rows, weights = P(AXES, None), P(("xhi", "z", "core"), None)
    placed = (
        rows,
        P(AXES, None, None),
        P(AXES, None, None),
        P(AXES),
        weights,
        rows,
        rows,
        rows,
        weights,
        weights,
        weights,
    )
    return jax.shard_map(body, mesh=fine, in_specs=placed, out_specs=rows, check_vma=False)
```

```python
import functools
import math

import jax
import jax.numpy as jnp
from jax import lax
from jax.experimental import pallas as pl
from jax.experimental.pallas import tpu as pltpu
from jax.sharding import Mesh
from jax.sharding import PartitionSpec as P

D = 7168
HS = 256
CAP = 8
NX = 2
NZ = 8
CHIPS = NX * NZ
ROWS = 16
AXES = ("y", "xlo", "xhi", "z", "core")
RING = ("xhi", "z")


def attend(queries, key_cache, value_cache, lengths):
    count_rows = queries.shape[0]
    cache_len = key_cache.shape[1]
    head_size = key_cache.shape[2]
    num_heads = queries.shape[1] // head_size
    grouped = queries.reshape(count_rows, num_heads, head_size)
    scores = jnp.einsum(
        "rhd,rld->rhl", grouped, key_cache, preferred_element_type=jnp.float32
    ) / math.sqrt(head_size)
    positions = lax.broadcasted_iota(jnp.int32, (1, 1, cache_len), 2)
    scores = jnp.where(positions < lengths[:, None, None], scores, -1e30)
    largest = jnp.max(scores, axis=2, keepdims=True)
    expo = jnp.exp(scores - largest)
    weights = (expo / jnp.sum(expo, axis=2, keepdims=True)).astype(jnp.bfloat16)
    mixed = jnp.einsum("rhl,rld->rhd", weights, value_cache, preferred_element_type=jnp.float32)
    return mixed.astype(jnp.bfloat16).reshape(count_rows, num_heads * head_size)


def swap_cores(a):
    return lax.ppermute(a, "core", [(0, 1), (1, 0)])


def swap_x(a):
    return lax.ppermute(a, "xhi", [(0, 1), (1, 0)])


def shift(a, by):
    return lax.ppermute(a, "z", [(i, (i + by) % NZ) for i in range(NZ)])


def add(*terms):
    total = terms[0].astype(jnp.float32)
    for term in terms[1:]:
        total = total + term.astype(jnp.float32)
    return total


def add16(*terms):
    return add(*terms).astype(jnp.bfloat16)


def sum_z(part):
    half = part[0].shape[-1] // 2
    up, down = shift(part[4][:, :half], 1), shift(part[4][:, half:], -1)
    up = shift(add_part(part[3], up, 0), 1)
    down = shift(add_part(part[5], down, half), -1)
    up = shift(add16(part[2], up), 1)
    down = shift(add16(part[6], down), -1)
    up = shift(add16(part[1], up), 1)
    down = shift(add16(part[7], down), -1)
    return add16(part[0], up, down)


def add_part(whole, piece, at):
    size = piece.shape[-1]
    added = add16(whole[:, at : at + size], piece)
    return jnp.concatenate([whole[:, :at], added, whole[:, at + size :]], axis=1)


def cut(part):
    both = part.shape[0] // NZ
    return [part[k * both : (k + 1) * both] for k in range(NZ)]


def gather_z(mine):
    half = mine.shape[-1] // 2
    a1, b1 = shift(mine, 1), shift(mine, -1)
    a2, b2 = shift(a1, 1), shift(b1, -1)
    a3, b3 = shift(a2, 1), shift(b2, -1)
    a4, b4 = shift(a3[..., :half], 1), shift(b3[..., half:], -1)
    return [mine, b1, b2, b3, a4, b4, a3, a2, a1]


def project_kernel(tile, place, a, w_own, w_oth, out):
    blocks = []
    for rz in range(NZ):
        for kind in range(a.shape[0]):
            for rx in range(NX):
                x = lax.rem(place[0] + rx, NX)
                z = lax.rem(place[1] + rz, NZ)
                blocks.append(a[kind, x * NZ + z].astype(jnp.float32))
    rows = jnp.concatenate(blocks, axis=0)
    depth = w_own.shape[0]
    first = place[2] == 0
    own = jnp.where(first, rows[:, :depth], rows[:, depth:]).astype(jnp.bfloat16)
    oth = jnp.where(first, rows[:, depth:], rows[:, :depth]).astype(jnp.bfloat16)
    for i in range(D // tile):
        at = slice(i * tile, (i + 1) * tile)
        total = jnp.dot(own, w_own[:, at], preferred_element_type=jnp.float32)
        total += jnp.dot(oth, w_oth[:, at], preferred_element_type=jnp.float32)
        out[:, at] = total.astype(jnp.bfloat16)


def project(place, attended, w_own, w_oth, tile=1024):
    rows = math.prod(attended.shape[:3])
    whole = pl.BlockSpec(memory_space=pltpu.VMEM)
    return pl.pallas_call(
        functools.partial(project_kernel, tile),
        out_shape=jax.ShapeDtypeStruct((rows, D), jnp.bfloat16),
        in_specs=[pl.BlockSpec(memory_space=pltpu.SMEM)] + [whole] * 3,
        out_specs=whole,
        compiler_params=pltpu.CompilerParams(vmem_limit_bytes=16 * 1024 * 1024),
        name="project",
    )(place, attended, w_own, w_oth)


def expert_kernel(tile, *refs):
    pieces, (g_own, g_oth, u_own, u_oth, d_own, d_oth, out, first, last, sems) = refs[:9], refs[9:]
    steps, units = D // tile, g_own.shape[0]
    dims = (((1,), (1,)), ((), ()))

    def copies(i):
        at = pl.ds(i * tile, tile)
        return [
            pltpu.make_async_copy(w.at[:, at], first.at[pl.ds(k * units, units), at], sems.at[i, k])
            for k, w in enumerate((g_own, g_oth, u_own, u_oth))
        ]

    down = [
        pltpu.make_async_copy(w, last.at[pl.ds(k * units, units)], sems.at[steps, k])
        for k, w in enumerate((d_own, d_oth))
    ]
    moves = [copies(i) for i in range(steps)]
    for move in moves:
        for copy in move:
            copy.start()
    for copy in down:
        copy.start()
    both = None
    for i in range(steps):
        lo, hi = i * tile, (i + 1) * tile
        if hi <= D // 2:
            far = pieces[4][:, lo:hi]
        else:
            far = pieces[5][:, lo - D // 2 : hi - D // 2]
        near = [p[:, lo:hi] for p in pieces[:4]]
        back = [p[:, lo:hi] for p in pieces[6:]]
        piece = jnp.concatenate(near + [far] + back, axis=0)
        for copy in moves[i]:
            copy.wait()
        term = lax.dot_general(piece, first[:, lo:hi], dims, preferred_element_type=jnp.float32)
        both = term if both is None else both + term
    gate, up = both[:, : 2 * units], both[:, 2 * units :]
    act = (gate / (1.0 + jnp.exp(-gate)) * up).astype(jnp.bfloat16)
    for copy in down:
        copy.wait()
    for i in range(steps):
        at = slice(i * tile, (i + 1) * tile)
        out[:, at] = jnp.dot(act, last[:, at], preferred_element_type=jnp.float32).astype(jnp.bfloat16)


def expert(pieces, weights, tile=896):
    units = weights[0].shape[0]
    whole = pl.BlockSpec(memory_space=pltpu.VMEM)
    return pl.pallas_call(
        functools.partial(expert_kernel, tile),
        out_shape=jax.ShapeDtypeStruct((CHIPS * CAP, D), jnp.bfloat16),
        in_specs=[whole] * len(pieces) + [pl.BlockSpec(memory_space=pl.ANY)] * len(weights),
        out_specs=whole,
        scratch_shapes=[
            pltpu.VMEM((4 * units, D), jnp.bfloat16),
            pltpu.VMEM((2 * units, D), jnp.bfloat16),
            pltpu.SemaphoreType.DMA((D // tile + 1, 4)),
        ],
        compiler_params=pltpu.CompilerParams(vmem_limit_bytes=52 * 1024 * 1024),
        name="expert",
    )(*pieces, *weights)


def slots(routes):
    named = jnp.any(routes == 0, axis=1)
    row = jnp.arange(ROWS)
    before = row[:, None] < row[None, :]
    n_named = jnp.sum(named)
    rank_named = jnp.sum((before & named[:, None]).astype(jnp.int32), axis=0)
    slot = jnp.where(named, rank_named, n_named + row - rank_named)
    return row[:, None] == slot[None, :]


def body(
    queries,
    key_cache,
    value_cache,
    lengths,
    out_proj,
    residual,
    routes,
    route_weight,
    w_gate,
    w_up,
    w_down,
):
    place = jnp.stack([lax.axis_index(a) for a in ("xhi", "z", "core")]).astype(jnp.int32)
    o_oth = swap_cores(out_proj)
    g_oth, u_oth, d_oth = swap_cores(w_gate), swap_cores(w_up), swap_cores(w_down)

    order = slots(routes)
    order16 = order.astype(jnp.bfloat16)
    share = jnp.sum(jnp.where(routes == 0, route_weight, 0.0), axis=1)
    share = jnp.sum(jnp.where(order, share[None, :], 0.0), axis=1)

    res = jnp.dot(order16, residual, preferred_element_type=jnp.float32)
    res_oth = swap_x(res[:CAP].astype(jnp.bfloat16))
    attended = attend(queries, key_cache, value_cache, lengths)
    attended = jnp.dot(order16, attended, preferred_element_type=jnp.float32).astype(jnp.bfloat16)
    by_heads = lax.all_to_all(
        attended.reshape(2, CAP, CHIPS, 2 * HS), RING, split_axis=2, concat_axis=1
    )
    by_heads, o_oth, g_oth, u_oth, d_oth, res_oth = lax.optimization_barrier(
        (by_heads, o_oth, g_oth, u_oth, d_oth, res_oth)
    )
    pair_res = jnp.concatenate([res[:CAP], res_oth.astype(jnp.float32)], axis=0)
    mine = sum_z(cut(project(place, by_heads, out_proj, o_oth)))

    theirs = swap_x(mine[: NX * CAP])
    pair = pair_res + add(mine[: NX * CAP], jnp.concatenate([theirs[CAP:], theirs[:CAP]], axis=0))
    normed = (
        pair * lax.rsqrt(jnp.mean(pair * pair, axis=1, keepdims=True) + 1e-06)
    ).astype(jnp.bfloat16)
    pieces = gather_z(normed)
    rows = expert(pieces, (w_gate, g_oth, w_up, u_oth, w_down, d_oth))
    got = sum_z(cut(rows))
    expert_rows = add(got[:CAP], swap_x(got[CAP:]))
    rest = mine[NX * CAP :]
    others = res[CAP:] + add(rest[:CAP], swap_x(rest[CAP:]))
    done = jnp.concatenate(
        [pair[:CAP] + share[:CAP, None] * expert_rows, others], axis=0
    ).astype(jnp.bfloat16)
    return jnp.dot(order16.T, done, preferred_element_type=jnp.float32).astype(jnp.bfloat16)


def solution(mesh):
    fine = Mesh(mesh.devices.reshape(4, 2, NX, NZ, 2), AXES)
    rows, weights = P(AXES, None), P(("xhi", "z", "core"), None)
    placed = (
        rows,
        P(AXES, None, None),
        P(AXES, None, None),
        P(AXES),
        weights,
        rows,
        rows,
        rows,
        weights,
        weights,
        weights,
    )
    return jax.shard_map(body, mesh=fine, in_specs=placed, out_specs=rows, check_vma=False)
```

```python
import functools
import math

import jax
import jax.numpy as jnp
from jax import lax
from jax.experimental import pallas as pl
from jax.experimental.pallas import tpu as pltpu
from jax.sharding import Mesh
from jax.sharding import PartitionSpec as P

D = 7168
HS = 256
CAP = 8
NX = 2
NZ = 8
CHIPS = NX * NZ
ROWS = 16
AXES = ("y", "xlo", "xhi", "z", "core")
RING = ("xhi", "z", "core")
TEAMS = [
    [(x * NZ + z) * 2 + (z + odd) % 2 for x in range(NX) for z in range(NZ)] for odd in range(2)
]


def attend(queries, key_cache, value_cache, lengths):
    count_rows = queries.shape[0]
    cache_len = key_cache.shape[1]
    head_size = key_cache.shape[2]
    num_heads = queries.shape[1] // head_size
    grouped = queries.reshape(count_rows, num_heads, head_size)
    scores = jnp.einsum(
        "rhd,rld->rhl", grouped, key_cache, preferred_element_type=jnp.float32
    ) / math.sqrt(head_size)
    positions = lax.broadcasted_iota(jnp.int32, (1, 1, cache_len), 2)
    scores = jnp.where(positions < lengths[:, None, None], scores, -1e30)
    largest = jnp.max(scores, axis=2, keepdims=True)
    expo = jnp.exp(scores - largest)
    weights = (expo / jnp.sum(expo, axis=2, keepdims=True)).astype(jnp.bfloat16)
    mixed = jnp.einsum("rhl,rld->rhd", weights, value_cache, preferred_element_type=jnp.float32)
    return mixed.astype(jnp.bfloat16).reshape(count_rows, num_heads * head_size)


def swap_cores(a):
    return lax.ppermute(a, "core", [(0, 1), (1, 0)])


def swap_x(a):
    return lax.ppermute(a, "xhi", [(0, 1), (1, 0)])


def shift(a, by):
    moves = [
        (2 * z + core, 2 * ((z + by) % NZ) + (core + by) % 2)
        for z in range(NZ)
        for core in range(2)
    ]
    return lax.ppermute(a, ("z", "core"), moves)


def add(*terms):
    total = terms[0].astype(jnp.float32)
    for term in terms[1:]:
        total = total + term.astype(jnp.float32)
    return total


def add16(*terms):
    return add(*terms).astype(jnp.bfloat16)


def sum_z(part):
    half = part[0].shape[-1] // 2
    up, down = shift(part[4][:, :half], 1), shift(part[4][:, half:], -1)
    up = shift(add_part(part[3], up, 0), 1)
    down = shift(add_part(part[5], down, half), -1)
    up = shift(add16(part[2], up), 1)
    down = shift(add16(part[6], down), -1)
    up = shift(add16(part[1], up), 1)
    down = shift(add16(part[7], down), -1)
    return add16(part[0], up, down)


def add_part(whole, piece, at):
    size = piece.shape[-1]
    added = add16(whole[:, at : at + size], piece)
    return jnp.concatenate([whole[:, :at], added, whole[:, at + size :]], axis=1)


def cut(part):
    both = part.shape[0] // NZ
    return [part[k * both : (k + 1) * both] for k in range(NZ)]


def gather_z(mine):
    half = mine.shape[-1] // 2
    a1, b1 = shift(mine, 1), shift(mine, -1)
    a2, b2 = shift(a1, 1), shift(b1, -1)
    a3, b3 = shift(a2, 1), shift(b2, -1)
    a4, b4 = shift(a3[..., :half], 1), shift(b3[..., half:], -1)
    return [mine, b1, b2, b3, a4, b4, a3, a2, a1]


def project_kernel(tile, place, a, w_own, w_oth, out, held, sems):
    steps, depth = D // tile, w_own.shape[0]
    moves = [
        [
            pltpu.make_async_copy(w.at[:, pl.ds(i * tile, tile)], held.at[k, i], sems.at[k, i])
            for k, w in enumerate((w_own, w_oth))
        ]
        for i in range(steps)
    ]
    for move in moves:
        for copy in move:
            copy.start()
    blocks = []
    for rz in range(NZ):
        for kind in range(a.shape[0]):
            for rx in range(NX):
                x = lax.rem(place[0] + rx, NX)
                z = lax.rem(place[1] + rz, NZ)
                blocks.append(a[kind, x * NZ + z].astype(jnp.float32))
    rows = jnp.concatenate(blocks, axis=0)
    first = place[2] == 0
    own = jnp.where(first, rows[:, :depth], rows[:, depth:]).astype(jnp.bfloat16)
    oth = jnp.where(first, rows[:, depth:], rows[:, :depth]).astype(jnp.bfloat16)
    for i in range(steps):
        for copy in moves[i]:
            copy.wait()
        total = jnp.dot(own, held[0, i], preferred_element_type=jnp.float32)
        total += jnp.dot(oth, held[1, i], preferred_element_type=jnp.float32)
        out[:, i * tile : (i + 1) * tile] = total.astype(jnp.bfloat16)


def project(place, attended, w_own, w_oth, tile=1024):
    rows, depth = math.prod(attended.shape[:3]), w_own.shape[0]
    whole = pl.BlockSpec(memory_space=pltpu.VMEM)
    anywhere = pl.BlockSpec(memory_space=pl.ANY)
    return pl.pallas_call(
        functools.partial(project_kernel, tile),
        out_shape=jax.ShapeDtypeStruct((rows, D), jnp.bfloat16),
        in_specs=[pl.BlockSpec(memory_space=pltpu.SMEM), whole, anywhere, anywhere],
        out_specs=whole,
        scratch_shapes=[
            pltpu.VMEM((2, D // tile, depth, tile), jnp.bfloat16),
            pltpu.SemaphoreType.DMA((2, D // tile)),
        ],
        compiler_params=pltpu.CompilerParams(vmem_limit_bytes=32 * 1024 * 1024),
        name="project",
    )(place, attended, w_own, w_oth)


def expert_kernel(tile, *refs):
    pieces, first, (d_own, d_oth, out) = refs[:9], refs[9:13], refs[13:]
    steps, units = D // tile, d_own.shape[0]
    dims = (((1,), (1,)), ((), ()))
    both = None
    for i in range(steps):
        lo, hi = i * tile, (i + 1) * tile
        if hi <= D // 2:
            far = pieces[4][:, lo:hi]
        else:
            far = pieces[5][:, lo - D // 2 : hi - D // 2]
        near = [p[:, lo:hi] for p in pieces[:4]]
        back = [p[:, lo:hi] for p in pieces[6:]]
        piece = jnp.concatenate(near + [far] + back, axis=0)
        weights = jnp.concatenate([w[:, lo:hi] for w in first], axis=0)
        term = lax.dot_general(piece, weights, dims, preferred_element_type=jnp.float32)
        both = term if both is None else both + term
    gate, up = both[:, : 2 * units], both[:, 2 * units :]
    act = (gate / (1.0 + jnp.exp(-gate)) * up).astype(jnp.bfloat16)
    for i in range(steps):
        at = slice(i * tile, (i + 1) * tile)
        last = jnp.concatenate([d_own[:, at], d_oth[:, at]], axis=0)
        out[:, at] = jnp.dot(act, last, preferred_element_type=jnp.float32).astype(jnp.bfloat16)


def expert(pieces, weights, tile=896):
    whole = pl.BlockSpec(memory_space=pltpu.VMEM)
    return pl.pallas_call(
        functools.partial(expert_kernel, tile),
        out_shape=jax.ShapeDtypeStruct((CHIPS * CAP, D), jnp.bfloat16),
        in_specs=[whole] * (len(pieces) + len(weights)),
        out_specs=whole,
        compiler_params=pltpu.CompilerParams(vmem_limit_bytes=16 * 1024 * 1024),
        name="expert",
    )(*pieces, *weights)


def slots(routes):
    named = jnp.any(routes == 0, axis=1)
    row = jnp.arange(ROWS)
    before = row[:, None] < row[None, :]
    n_named = jnp.sum(named)
    rank_named = jnp.sum((before & named[:, None]).astype(jnp.int32), axis=0)
    slot = jnp.where(named, rank_named, n_named + row - rank_named)
    return row[:, None] == slot[None, :]


def body(
    queries,
    key_cache,
    value_cache,
    lengths,
    out_proj,
    residual,
    routes,
    route_weight,
    w_gate,
    w_up,
    w_down,
):
    place = jnp.stack([lax.axis_index(a) for a in ("xhi", "z", "core")]).astype(jnp.int32)
    o_oth = swap_cores(out_proj)

    order = slots(routes)
    order16 = order.astype(jnp.bfloat16)
    share = jnp.sum(jnp.where(routes == 0, route_weight, 0.0), axis=1)
    share = jnp.sum(jnp.where(order, share[None, :], 0.0), axis=1)

    res = jnp.dot(order16, residual, preferred_element_type=jnp.float32)
    res_oth = swap_x(res[:CAP].astype(jnp.bfloat16))
    attended = attend(queries, key_cache, value_cache, lengths)
    attended = jnp.dot(order16, attended, preferred_element_type=jnp.float32).astype(jnp.bfloat16)
    by_heads = lax.all_to_all(
        attended.reshape(2, CAP, CHIPS, 2 * HS), RING, split_axis=2, concat_axis=1,
        axis_index_groups=TEAMS,
    )
    by_heads, o_oth, res_oth, w_gate, w_up, w_down = lax.optimization_barrier(
        (by_heads, o_oth, res_oth, w_gate, w_up, w_down)
    )
    g_oth, u_oth, d_oth = swap_cores(w_gate), swap_cores(w_up), swap_cores(w_down)
    pair_res = jnp.concatenate([res[:CAP], res_oth.astype(jnp.float32)], axis=0)
    mine = sum_z(cut(project(place, by_heads, out_proj, o_oth)))

    theirs = swap_x(mine[: NX * CAP])
    pair = pair_res + add(mine[: NX * CAP], jnp.concatenate([theirs[CAP:], theirs[:CAP]], axis=0))
    normed = (
        pair * lax.rsqrt(jnp.mean(pair * pair, axis=1, keepdims=True) + 1e-06)
    ).astype(jnp.bfloat16)
    pieces = gather_z(normed)
    rows = expert(pieces, (w_gate, g_oth, w_up, u_oth, w_down, d_oth))
    got = sum_z(cut(rows))
    expert_rows = add(got[:CAP], swap_x(got[CAP:]))
    rest = mine[NX * CAP :]
    others = res[CAP:] + add(rest[:CAP], swap_x(rest[CAP:]))
    done = jnp.concatenate(
        [pair[:CAP] + share[:CAP, None] * expert_rows, others], axis=0
    ).astype(jnp.bfloat16)
    return jnp.dot(order16.T, done, preferred_element_type=jnp.float32).astype(jnp.bfloat16)


def solution(mesh):
    fine = Mesh(mesh.devices.reshape(4, 2, NX, NZ, 2), AXES)
    rows, weights = P(AXES, None), P(("xhi", "z", "core"), None)
    placed = (
        rows,
        P(AXES, None, None),
        P(AXES, None, None),
        P(AXES),
        weights,
        rows,
        rows,
        rows,
        weights,
        weights,
        weights,
    )
    return jax.shard_map(body, mesh=fine, in_specs=placed, out_specs=rows, check_vma=False)
```

```python
import functools
import math

import jax
import jax.numpy as jnp
from jax import lax
from jax.experimental import pallas as pl
from jax.experimental.pallas import tpu as pltpu
from jax.sharding import Mesh
from jax.sharding import PartitionSpec as P

D = 7168
HS = 256
CAP = 8
NX = 2
NZ = 8
CHIPS = NX * NZ
ROWS = 16
AXES = ("y", "xlo", "xhi", "z", "core")
RING = ("xhi", "z")


def attend(queries, key_cache, value_cache, lengths):
    count_rows = queries.shape[0]
    cache_len = key_cache.shape[1]
    head_size = key_cache.shape[2]
    num_heads = queries.shape[1] // head_size
    grouped = queries.reshape(count_rows, num_heads, head_size)
    scores = jnp.einsum(
        "rhd,rld->rhl", grouped, key_cache, preferred_element_type=jnp.float32
    ) / math.sqrt(head_size)
    positions = lax.broadcasted_iota(jnp.int32, (1, 1, cache_len), 2)
    scores = jnp.where(positions < lengths[:, None, None], scores, -1e30)
    largest = jnp.max(scores, axis=2, keepdims=True)
    expo = jnp.exp(scores - largest)
    weights = (expo / jnp.sum(expo, axis=2, keepdims=True)).astype(jnp.bfloat16)
    mixed = jnp.einsum("rhl,rld->rhd", weights, value_cache, preferred_element_type=jnp.float32)
    return mixed.astype(jnp.bfloat16).reshape(count_rows, num_heads * head_size)


def swap_cores(a):
    return lax.ppermute(a, "core", [(0, 1), (1, 0)])


def swap_x(a):
    return lax.ppermute(a, "xhi", [(0, 1), (1, 0)])


def shift(a, by):
    return lax.ppermute(a, "z", [(i, (i + by) % NZ) for i in range(NZ)])


def add(*terms):
    total = terms[0].astype(jnp.float32)
    for term in terms[1:]:
        total = total + term.astype(jnp.float32)
    return total


def add16(*terms):
    return add(*terms).astype(jnp.bfloat16)


def sum_z(part, beside=None):
    half = part[0].shape[-1] // 2
    up, down = shift(part[4][:, :half], 1), shift(part[4][:, half:], -1)
    up = shift(add_part(part[3], up, 0), 1)
    down = shift(add_part(part[5], down, half), -1)
    up = shift(add16(part[2], up), 1)
    down = shift(add16(part[6], down), -1)
    if beside is not None:
        up, down, beside = lax.optimization_barrier((up, down, beside))
    up = shift(add16(part[1], up), 1)
    down = shift(add16(part[7], down), -1)
    return add16(part[0], up, down), beside


def add_part(whole, piece, at):
    size = piece.shape[-1]
    added = add16(whole[:, at : at + size], piece)
    return jnp.concatenate([whole[:, :at], added, whole[:, at + size :]], axis=1)


def cut(part):
    both = part.shape[0] // NZ
    return [part[k * both : (k + 1) * both] for k in range(NZ)]


def gather_z(mine):
    half = mine.shape[-1] // 2
    a1, b1 = shift(mine, 1), shift(mine, -1)
    a2, b2 = shift(a1, 1), shift(b1, -1)
    a3, b3 = shift(a2, 1), shift(b2, -1)
    a4, b4 = shift(a3[..., :half], 1), shift(b3[..., half:], -1)
    return [mine, b1, b2, b3, a4, b4, a3, a2, a1]


def project_kernel(tile, place, a, w_own, w_oth, out, near, far, held, sems):
    steps, depth = D // tile, w_own.shape[0]
    moves = [
        [
            pltpu.make_async_copy(w.at[:, pl.ds(i * tile, tile)], held.at[k, i], sems.at[k, i])
            for k, w in enumerate((w_own, w_oth))
        ]
        for i in range(steps)
    ]
    for move in moves:
        for copy in move:
            copy.start()
    pairs = [(rx, rz) for rx in range(NX) for rz in range(NZ)]
    blocks = []
    for kind, order in enumerate((sorted(pairs, key=lambda p: p[1]), pairs)):
        for rx, rz in order:
            x = lax.rem(place[0] + rx, NX)
            z = lax.rem(place[1] + rz, NZ)
            blocks.append(a[kind, x * NZ + z].astype(jnp.float32))
    rows = jnp.concatenate(blocks, axis=0)
    first = place[2] == 0
    own = jnp.where(first, rows[:, :depth], rows[:, depth:]).astype(jnp.bfloat16)
    oth = jnp.where(first, rows[:, depth:], rows[:, :depth]).astype(jnp.bfloat16)
    for i in range(steps):
        for copy in moves[i]:
            copy.wait()
        total = jnp.dot(own, held[0, i], preferred_element_type=jnp.float32)
        total += jnp.dot(oth, held[1, i], preferred_element_type=jnp.float32)
        total = total.astype(jnp.bfloat16)
        at = slice(i * tile, (i + 1) * tile)
        top, middle = out.shape[0], out.shape[0] + near.shape[0]
        out[:, at], near[:, at], far[:, at] = total[:top], total[top:middle], total[middle:]


def project(place, attended, w_own, w_oth, tile=1024):
    rows, depth = CHIPS * attended.shape[2], w_own.shape[0]
    whole = pl.BlockSpec(memory_space=pltpu.VMEM)
    anywhere = pl.BlockSpec(memory_space=pl.ANY)
    return pl.pallas_call(
        functools.partial(project_kernel, tile),
        out_shape=[
            jax.ShapeDtypeStruct((n, D), jnp.bfloat16) for n in (rows, rows // NX, rows // NX)
        ],
        in_specs=[pl.BlockSpec(memory_space=pltpu.SMEM), whole, anywhere, anywhere],
        out_specs=[whole] * 3,
        scratch_shapes=[
            pltpu.VMEM((2, D // tile, depth, tile), jnp.bfloat16),
            pltpu.SemaphoreType.DMA((2, D // tile)),
        ],
        compiler_params=pltpu.CompilerParams(vmem_limit_bytes=58 * 1024 * 1024),
        name="project",
    )(place, attended, w_own, w_oth)


def expert_kernel(tile, *refs):
    pieces, first, (d_own, d_oth, out) = refs[:9], refs[9:13], refs[13:]
    steps, units = D // tile, d_own.shape[0]
    dims = (((1,), (1,)), ((), ()))
    both = None
    for i in range(steps):
        lo, hi = i * tile, (i + 1) * tile
        if hi <= D // 2:
            far = pieces[4][:, lo:hi]
        else:
            far = pieces[5][:, lo - D // 2 : hi - D // 2]
        near = [p[:, lo:hi] for p in pieces[:4]]
        back = [p[:, lo:hi] for p in pieces[6:]]
        piece = jnp.concatenate(near + [far] + back, axis=0)
        weights = jnp.concatenate([w[:, lo:hi] for w in first], axis=0)
        term = lax.dot_general(piece, weights, dims, preferred_element_type=jnp.float32)
        both = term if both is None else both + term
    gate, up = both[:, : 2 * units], both[:, 2 * units :]
    act = (gate / (1.0 + jnp.exp(-gate)) * up).astype(jnp.bfloat16)
    for i in range(steps):
        at = slice(i * tile, (i + 1) * tile)
        last = jnp.concatenate([d_own[:, at], d_oth[:, at]], axis=0)
        out[:, at] = jnp.dot(act, last, preferred_element_type=jnp.float32).astype(jnp.bfloat16)


def expert(pieces, weights, tile=896):
    whole = pl.BlockSpec(memory_space=pltpu.VMEM)
    return pl.pallas_call(
        functools.partial(expert_kernel, tile),
        out_shape=jax.ShapeDtypeStruct((CHIPS * CAP, D), jnp.bfloat16),
        in_specs=[whole] * (len(pieces) + len(weights)),
        out_specs=whole,
        compiler_params=pltpu.CompilerParams(vmem_limit_bytes=16 * 1024 * 1024),
        name="expert",
    )(*pieces, *weights)


def slots(routes):
    named = jnp.any(routes == 0, axis=1)
    row = jnp.arange(ROWS)
    before = row[:, None] < row[None, :]
    n_named = jnp.sum(named)
    rank_named = jnp.sum((before & named[:, None]).astype(jnp.int32), axis=0)
    slot = jnp.where(named, rank_named, n_named + row - rank_named)
    return row[:, None] == slot[None, :]


def body(
    queries,
    key_cache,
    value_cache,
    lengths,
    out_proj,
    residual,
    routes,
    route_weight,
    w_gate,
    w_up,
    w_down,
):
    place = jnp.stack([lax.axis_index(a) for a in ("xhi", "z", "core")]).astype(jnp.int32)
    o_oth = swap_cores(out_proj)

    order = slots(routes)
    order16 = order.astype(jnp.bfloat16)
    share = jnp.sum(jnp.where(routes == 0, route_weight, 0.0), axis=1)
    share = jnp.sum(jnp.where(order, share[None, :], 0.0), axis=1)

    res = jnp.dot(order16, residual, preferred_element_type=jnp.float32)
    attended = attend(queries, key_cache, value_cache, lengths)
    attended = jnp.dot(order16, attended, preferred_element_type=jnp.float32).astype(jnp.bfloat16)
    by_heads = lax.all_to_all(
        attended.reshape(2, CAP, CHIPS, 2 * HS), RING, split_axis=2, concat_axis=1
    )
    by_heads, o_oth, w_gate, w_up, w_down = lax.optimization_barrier(
        (by_heads, o_oth, w_gate, w_up, w_down)
    )
    g_oth, u_oth, d_oth = swap_cores(w_gate), swap_cores(w_up), swap_cores(w_down)
    parts, near, far = project(place, by_heads, out_proj, o_oth)
    mine, far = sum_z(cut(parts), swap_x(far))
    rest = add16(near, far)

    chosen = add(res[:CAP], mine[:CAP])
    mine = jnp.concatenate([chosen.astype(jnp.bfloat16), mine[CAP:]], axis=0)
    theirs = swap_x(mine)
    chosen = add(chosen, theirs[CAP:])
    pair = add(mine, jnp.concatenate([theirs[CAP:], theirs[:CAP]], axis=0))
    normed = (
        pair * lax.rsqrt(jnp.mean(pair * pair, axis=1, keepdims=True) + 1e-06)
    ).astype(jnp.bfloat16)
    pieces = gather_z(normed)
    rows = expert(pieces, (w_gate, g_oth, w_up, u_oth, w_down, d_oth))
    both = [jnp.concatenate(p, axis=0) for p in zip(cut(rows), cut(rest))]
    got, _ = sum_z(both)
    expert_rows = add(got[:CAP], swap_x(got[CAP : NX * CAP]))
    others = add(res[CAP:], got[NX * CAP :])
    done = jnp.concatenate(
        [chosen + share[:CAP, None] * expert_rows, others], axis=0
    ).astype(jnp.bfloat16)
    return jnp.dot(order16.T, done, preferred_element_type=jnp.float32).astype(jnp.bfloat16)


def solution(mesh):
    fine = Mesh(mesh.devices.reshape(4, 2, NX, NZ, 2), AXES)
    rows, weights = P(AXES, None), P(("xhi", "z", "core"), None)
    placed = (
        rows,
        P(AXES, None, None),
        P(AXES, None, None),
        P(AXES),
        weights,
        rows,
        rows,
        rows,
        weights,
        weights,
        weights,
    )
    return jax.shard_map(body, mesh=fine, in_specs=placed, out_specs=rows, check_vma=False)
```

```python
import functools
import math

import jax
import jax.numpy as jnp
from jax import lax
from jax.experimental import pallas as pl
from jax.experimental.pallas import tpu as pltpu
from jax.sharding import Mesh
from jax.sharding import PartitionSpec as P

D = 7168
HS = 256
CAP = 8
NX = 2
NZ = 8
CHIPS = NX * NZ
ROWS = 16
AXES = ("y", "xlo", "xhi", "z", "core")
RING = ("xhi", "z")


def attend(queries, key_cache, value_cache, lengths):
    count_rows = queries.shape[0]
    cache_len = key_cache.shape[1]
    head_size = key_cache.shape[2]
    num_heads = queries.shape[1] // head_size
    grouped = queries.reshape(count_rows, num_heads, head_size)
    scores = jnp.einsum(
        "rhd,rld->rhl", grouped, key_cache, preferred_element_type=jnp.float32
    ) / math.sqrt(head_size)
    positions = lax.broadcasted_iota(jnp.int32, (1, 1, cache_len), 2)
    scores = jnp.where(positions < lengths[:, None, None], scores, -1e30)
    largest = jnp.max(scores, axis=2, keepdims=True)
    expo = jnp.exp(scores - largest)
    weights = (expo / jnp.sum(expo, axis=2, keepdims=True)).astype(jnp.bfloat16)
    mixed = jnp.einsum("rhl,rld->rhd", weights, value_cache, preferred_element_type=jnp.float32)
    return mixed.astype(jnp.bfloat16).reshape(count_rows, num_heads * head_size)


def swap_cores(a):
    return lax.ppermute(a, "core", [(0, 1), (1, 0)])


def swap_x(a):
    return lax.ppermute(a, "xhi", [(0, 1), (1, 0)])


def shift(a, by):
    return lax.ppermute(a, "z", [(i, (i + by) % NZ) for i in range(NZ)])


def add(*terms):
    total = terms[0].astype(jnp.float32)
    for term in terms[1:]:
        total = total + term.astype(jnp.float32)
    return total


def add16(*terms):
    return add(*terms).astype(jnp.bfloat16)


def sum_z(part, early=None, late=None):
    half = part[0].shape[-1] // 2
    up, down = shift(part[4][:, :half], 1), shift(part[4][:, half:], -1)
    up = shift(add_part(part[3], up, 0), 1)
    down = shift(add_part(part[5], down, half), -1)
    if early is not None:
        up, down, early = lax.optimization_barrier((up, down, early))
    up = shift(add16(part[2], up), 1)
    down = shift(add16(part[6], down), -1)
    up = shift(add16(part[1], up), 1)
    down = shift(add16(part[7], down), -1)
    if late is not None:
        up, down, late = lax.optimization_barrier((up, down, late))
    return add16(part[0], up, down), early, late


def add_part(whole, piece, at):
    size = piece.shape[-1]
    added = add16(whole[:, at : at + size], piece)
    return jnp.concatenate([whole[:, :at], added, whole[:, at + size :]], axis=1)


def cut(part):
    both = part.shape[0] // NZ
    return [part[k * both : (k + 1) * both] for k in range(NZ)]


def gather_z(mine):
    half = mine.shape[-1] // 2
    a1, b1 = shift(mine, 1), shift(mine, -1)
    a2, b2 = shift(a1, 1), shift(b1, -1)
    a3, b3 = shift(a2, 1), shift(b2, -1)
    a4, b4 = shift(a3[..., :half], 1), shift(b3[..., half:], -1)
    return [mine, b1, b2, b3, a4, b4, a3, a2, a1]


def project_kernel(tile, place, a, w_own, w_oth, out, near, far, held, sems):
    steps, depth = D // tile, w_own.shape[0]
    moves = [
        [
            pltpu.make_async_copy(w.at[:, pl.ds(i * tile, tile)], held.at[k, i], sems.at[k, i])
            for k, w in enumerate((w_own, w_oth))
        ]
        for i in range(steps)
    ]
    for move in moves:
        for copy in move:
            copy.start()
    pairs = [(rx, rz) for rx in range(NX) for rz in range(NZ)]
    blocks = []
    for kind, order in enumerate((sorted(pairs, key=lambda p: p[1]), pairs)):
        for rx, rz in order:
            x = lax.rem(place[0] + rx, NX)
            z = lax.rem(place[1] + rz, NZ)
            block = a[x * NZ + z].astype(jnp.float32)
            blocks.append(block[kind * CAP : (kind + 1) * CAP])
    rows = jnp.concatenate(blocks, axis=0)
    first = place[2] == 0
    own = jnp.where(first, rows[:, :depth], rows[:, depth:]).astype(jnp.bfloat16)
    oth = jnp.where(first, rows[:, depth:], rows[:, :depth]).astype(jnp.bfloat16)
    for i in range(steps):
        for copy in moves[i]:
            copy.wait()
        total = jnp.dot(own, held[0, i], preferred_element_type=jnp.float32)
        total += jnp.dot(oth, held[1, i], preferred_element_type=jnp.float32)
        total = total.astype(jnp.bfloat16)
        at = slice(i * tile, (i + 1) * tile)
        top, middle = out.shape[0], out.shape[0] + near.shape[0]
        out[:, at], near[:, at], far[:, at] = total[:top], total[top:middle], total[middle:]


def project(place, attended, w_own, w_oth, tile=1024):
    rows, depth = CHIPS * CAP, w_own.shape[0]
    whole = pl.BlockSpec(memory_space=pltpu.VMEM)
    anywhere = pl.BlockSpec(memory_space=pl.ANY)
    return pl.pallas_call(
        functools.partial(project_kernel, tile),
        out_shape=[
            jax.ShapeDtypeStruct((n, D), jnp.bfloat16) for n in (rows, rows // NX, rows // NX)
        ],
        in_specs=[pl.BlockSpec(memory_space=pltpu.SMEM), whole, anywhere, anywhere],
        out_specs=[whole] * 3,
        scratch_shapes=[
            pltpu.VMEM((2, D // tile, depth, tile), jnp.bfloat16),
            pltpu.SemaphoreType.DMA((2, D // tile)),
        ],
        compiler_params=pltpu.CompilerParams(vmem_limit_bytes=50 * 1024 * 1024),
        cost_estimate=pl.CostEstimate(
            flops=8 * rows * depth * D, bytes_accessed=6 * depth * D, transcendentals=0
        ),
        name="project",
    )(place, attended, w_own, w_oth)


def expert_kernel(tile, *refs):
    pieces, first, (d_own, d_oth, out) = refs[:9], refs[9:13], refs[13:]
    steps, units = D // tile, d_own.shape[0]
    dims = (((1,), (1,)), ((), ()))
    both = None
    for i in range(steps):
        lo, hi = i * tile, (i + 1) * tile
        if hi <= D // 2:
            far = pieces[4][:, lo:hi]
        else:
            far = pieces[5][:, lo - D // 2 : hi - D // 2]
        near = [p[:, lo:hi] for p in pieces[:4]]
        back = [p[:, lo:hi] for p in pieces[6:]]
        piece = jnp.concatenate(near + [far] + back, axis=0)
        weights = jnp.concatenate([w[:, lo:hi] for w in first], axis=0)
        term = lax.dot_general(piece, weights, dims, preferred_element_type=jnp.float32)
        both = term if both is None else both + term
    gate, up = both[:, : 2 * units], both[:, 2 * units :]
    act = (gate / (1.0 + jnp.exp(-gate)) * up).astype(jnp.bfloat16)
    for i in range(steps):
        at = slice(i * tile, (i + 1) * tile)
        last = jnp.concatenate([d_own[:, at], d_oth[:, at]], axis=0)
        out[:, at] = jnp.dot(act, last, preferred_element_type=jnp.float32).astype(jnp.bfloat16)


def expert(pieces, weights, tile=896):
    whole = pl.BlockSpec(memory_space=pltpu.VMEM)
    return pl.pallas_call(
        functools.partial(expert_kernel, tile),
        out_shape=jax.ShapeDtypeStruct((CHIPS * CAP, D), jnp.bfloat16),
        in_specs=[whole] * (len(pieces) + len(weights)),
        out_specs=whole,
        compiler_params=pltpu.CompilerParams(vmem_limit_bytes=16 * 1024 * 1024),
        name="expert",
    )(*pieces, *weights)


def slots(routes):
    named = jnp.any(routes == 0, axis=1)
    row = jnp.arange(ROWS)
    before = row[:, None] < row[None, :]
    n_named = jnp.sum(named)
    rank_named = jnp.sum((before & named[:, None]).astype(jnp.int32), axis=0)
    slot = jnp.where(named, rank_named, n_named + row - rank_named)
    return row[:, None] == slot[None, :]


def body(
    queries,
    key_cache,
    value_cache,
    lengths,
    out_proj,
    residual,
    routes,
    route_weight,
    w_gate,
    w_up,
    w_down,
):
    place = jnp.stack([lax.axis_index(a) for a in ("xhi", "z", "core")]).astype(jnp.int32)
    o_oth = swap_cores(out_proj)

    order = slots(routes)
    order16 = order.astype(jnp.bfloat16)
    share = jnp.sum(jnp.where(routes == 0, route_weight, 0.0), axis=1)
    share = jnp.sum(jnp.where(order, share[None, :], 0.0), axis=1)

    res = jnp.dot(order16, residual, preferred_element_type=jnp.float32)
    attended = attend(queries, key_cache, value_cache, lengths)
    attended = jnp.dot(order16, attended, preferred_element_type=jnp.float32).astype(jnp.bfloat16)
    by_heads = lax.all_to_all(
        attended.reshape(ROWS, CHIPS, 2 * HS), RING, split_axis=1, concat_axis=0
    )
    by_heads, o_oth, w_gate, w_up, w_down = lax.optimization_barrier(
        (by_heads, o_oth, w_gate, w_up, w_down)
    )
    g_oth, u_oth, d_oth = swap_cores(w_gate), swap_cores(w_up), swap_cores(w_down)
    parts, near, far = project(place, by_heads, out_proj, o_oth)
    half = far.shape[0] // 2
    mine, first, second = sum_z(cut(parts), swap_x(far[:half]), swap_x(far[half:]))
    rest = add16(near, jnp.concatenate([first, second], axis=0))

    chosen = add(res[:CAP], mine[:CAP])
    mine = jnp.concatenate([chosen.astype(jnp.bfloat16), mine[CAP:]], axis=0)
    theirs = swap_x(mine)
    chosen = add(chosen, theirs[CAP:])
    pair = add(mine, jnp.concatenate([theirs[CAP:], theirs[:CAP]], axis=0))
    normed = (
        pair * lax.rsqrt(jnp.mean(pair * pair, axis=1, keepdims=True) + 1e-06)
    ).astype(jnp.bfloat16)
    pieces = gather_z(normed)
    rows = expert(pieces, (w_gate, g_oth, w_up, u_oth, w_down, d_oth))
    both = [jnp.concatenate(p, axis=0) for p in zip(cut(rows), cut(rest))]
    got, _, _ = sum_z(both)
    expert_rows = add(got[:CAP], swap_x(got[CAP : NX * CAP]))
    others = add(res[CAP:], got[NX * CAP :])
    done = jnp.concatenate(
        [chosen + share[:CAP, None] * expert_rows, others], axis=0
    ).astype(jnp.bfloat16)
    return jnp.dot(order16.T, done, preferred_element_type=jnp.float32).astype(jnp.bfloat16)


def solution(mesh):
    fine = Mesh(mesh.devices.reshape(4, 2, NX, NZ, 2), AXES)
    rows, weights = P(AXES, None), P(("xhi", "z", "core"), None)
    placed = (
        rows,
        P(AXES, None, None),
        P(AXES, None, None),
        P(AXES),
        weights,
        rows,
        rows,
        rows,
        weights,
        weights,
        weights,
    )
    return jax.shard_map(body, mesh=fine, in_specs=placed, out_specs=rows, check_vma=False)
```

```python
import functools
import math

import jax
import jax.numpy as jnp
from jax import lax
from jax.experimental import pallas as pl
from jax.experimental.pallas import tpu as pltpu
from jax.sharding import Mesh
from jax.sharding import PartitionSpec as P

D = 7168
HS = 256
CAP = 8
NX = 2
NZ = 8
CHIPS = NX * NZ
ROWS = 16
AXES = ("y", "xlo", "xhi", "z", "core")
RING = ("xhi", "z")


def attend(queries, key_cache, value_cache, lengths):
    count_rows = queries.shape[0]
    cache_len = key_cache.shape[1]
    head_size = key_cache.shape[2]
    num_heads = queries.shape[1] // head_size
    grouped = queries.reshape(count_rows, num_heads, head_size)
    scores = jnp.einsum(
        "rhd,rld->rhl", grouped, key_cache, preferred_element_type=jnp.float32
    ) / math.sqrt(head_size)
    positions = lax.broadcasted_iota(jnp.int32, (1, 1, cache_len), 2)
    scores = jnp.where(positions < lengths[:, None, None], scores, -1e30)
    largest = jnp.max(scores, axis=2, keepdims=True)
    expo = jnp.exp(scores - largest)
    weights = (expo / jnp.sum(expo, axis=2, keepdims=True)).astype(jnp.bfloat16)
    mixed = jnp.einsum("rhl,rld->rhd", weights, value_cache, preferred_element_type=jnp.float32)
    return mixed.astype(jnp.bfloat16).reshape(count_rows, num_heads * head_size)


def swap_cores(a):
    return lax.ppermute(a, "core", [(0, 1), (1, 0)])


def swap_x(a):
    return lax.ppermute(a, "xhi", [(0, 1), (1, 0)])


def shift(a, by):
    return lax.ppermute(a, "z", [(i, (i + by) % NZ) for i in range(NZ)])


def add(*terms):
    total = terms[0].astype(jnp.float32)
    for term in terms[1:]:
        total = total + term.astype(jnp.float32)
    return total


def add16(*terms):
    return add(*terms).astype(jnp.bfloat16)


def sum_z(part, early=None, late=None):
    half = part[0].shape[-1] // 2
    left, right = [p[:, :half] for p in part], [p[:, half:] for p in part]
    a, b = shift(left[4], 1), shift(right[4], -1)
    c, d = shift(right[3], 1), shift(left[5], -1)
    a, b = shift(add16(left[3], a), 1), shift(add16(right[5], b), -1)
    c, d = shift(add16(right[2], c), 1), shift(add16(left[6], d), -1)
    if early is not None:
        a, b, c, d, early = lax.optimization_barrier((a, b, c, d, early))
    a, b = shift(add16(left[2], a), 1), shift(add16(right[6], b), -1)
    c, d = shift(add16(right[1], c), 1), shift(add16(left[7], d), -1)
    a, b = shift(add16(left[1], a), 1), shift(add16(right[7], b), -1)
    if late is not None:
        a, b, c, d, late = lax.optimization_barrier((a, b, c, d, late))
    total = jnp.concatenate([add16(left[0], a, d), add16(right[0], b, c)], axis=1)
    return total, early, late


def cut(part):
    both = part.shape[0] // NZ
    return [part[k * both : (k + 1) * both] for k in range(NZ)]


def gather_z(mine):
    half = mine.shape[-1] // 2
    a1, b1 = shift(mine, 1), shift(mine, -1)
    a2, b2 = shift(a1, 1), shift(b1, -1)
    a3, b3 = shift(a2, 1), shift(b2, -1)
    a4, b4 = shift(a3[..., :half], 1), shift(b3[..., half:], -1)
    return [mine, b1, b2, b3, a4, b4, a3, a2, a1]


def project_kernel(tile, place, a, w_own, w_oth, out, near, far, held, sems):
    steps, depth = D // tile, w_own.shape[0]
    moves = [
        [
            pltpu.make_async_copy(w.at[:, pl.ds(i * tile, tile)], held.at[k, i], sems.at[k, i])
            for k, w in enumerate((w_own, w_oth))
        ]
        for i in range(steps)
    ]
    for move in moves:
        for copy in move:
            copy.start()
    pairs = [(rx, rz) for rx in range(NX) for rz in range(NZ)]
    blocks = []
    for kind, order in enumerate((sorted(pairs, key=lambda p: p[1]), pairs)):
        for rx, rz in order:
            x = lax.rem(place[0] + rx, NX)
            z = lax.rem(place[1] + rz, NZ)
            block = a[x * NZ + z].astype(jnp.float32)
            blocks.append(block[kind * CAP : (kind + 1) * CAP])
    rows = jnp.concatenate(blocks, axis=0)
    first = place[2] == 0
    own = jnp.where(first, rows[:, :depth], rows[:, depth:]).astype(jnp.bfloat16)
    oth = jnp.where(first, rows[:, depth:], rows[:, :depth]).astype(jnp.bfloat16)
    for i in range(steps):
        for copy in moves[i]:
            copy.wait()
        total = jnp.dot(own, held[0, i], preferred_element_type=jnp.float32)
        total += jnp.dot(oth, held[1, i], preferred_element_type=jnp.float32)
        total = total.astype(jnp.bfloat16)
        at = slice(i * tile, (i + 1) * tile)
        top, middle = out.shape[0], out.shape[0] + near.shape[0]
        out[:, at], near[:, at], far[:, at] = total[:top], total[top:middle], total[middle:]


def project(place, attended, w_own, w_oth, tile=1024):
    rows, depth = CHIPS * CAP, w_own.shape[0]
    whole = pl.BlockSpec(memory_space=pltpu.VMEM)
    anywhere = pl.BlockSpec(memory_space=pl.ANY)
    return pl.pallas_call(
        functools.partial(project_kernel, tile),
        out_shape=[
            jax.ShapeDtypeStruct((n, D), jnp.bfloat16) for n in (rows, rows // NX, rows // NX)
        ],
        in_specs=[pl.BlockSpec(memory_space=pltpu.SMEM), whole, anywhere, anywhere],
        out_specs=[whole] * 3,
        scratch_shapes=[
            pltpu.VMEM((2, D // tile, depth, tile), jnp.bfloat16),
            pltpu.SemaphoreType.DMA((2, D // tile)),
        ],
        compiler_params=pltpu.CompilerParams(vmem_limit_bytes=50 * 1024 * 1024),
        cost_estimate=pl.CostEstimate(
            flops=8 * rows * depth * D, bytes_accessed=6 * depth * D, transcendentals=0
        ),
        name="project",
    )(place, attended, w_own, w_oth)


def expert_kernel(tile, *refs):
    pieces, first, (d_own, d_oth, out) = refs[:9], refs[9:13], refs[13:]
    steps, units = D // tile, d_own.shape[0]
    dims = (((1,), (1,)), ((), ()))
    both = None
    for i in range(steps):
        lo, hi = i * tile, (i + 1) * tile
        if hi <= D // 2:
            far = pieces[4][:, lo:hi]
        else:
            far = pieces[5][:, lo - D // 2 : hi - D // 2]
        near = [p[:, lo:hi] for p in pieces[:4]]
        back = [p[:, lo:hi] for p in pieces[6:]]
        piece = jnp.concatenate(near + [far] + back, axis=0)
        weights = jnp.concatenate([w[:, lo:hi] for w in first], axis=0)
        term = lax.dot_general(piece, weights, dims, preferred_element_type=jnp.float32)
        both = term if both is None else both + term
    gate, up = both[:, : 2 * units], both[:, 2 * units :]
    act = (gate / (1.0 + jnp.exp(-gate)) * up).astype(jnp.bfloat16)
    for i in range(steps):
        at = slice(i * tile, (i + 1) * tile)
        last = jnp.concatenate([d_own[:, at], d_oth[:, at]], axis=0)
        out[:, at] = jnp.dot(act, last, preferred_element_type=jnp.float32).astype(jnp.bfloat16)


def expert(pieces, weights, tile=896):
    whole = pl.BlockSpec(memory_space=pltpu.VMEM)
    return pl.pallas_call(
        functools.partial(expert_kernel, tile),
        out_shape=jax.ShapeDtypeStruct((CHIPS * CAP, D), jnp.bfloat16),
        in_specs=[whole] * (len(pieces) + len(weights)),
        out_specs=whole,
        compiler_params=pltpu.CompilerParams(vmem_limit_bytes=16 * 1024 * 1024),
        name="expert",
    )(*pieces, *weights)


def slots(routes):
    named = jnp.any(routes == 0, axis=1)
    row = jnp.arange(ROWS)
    before = row[:, None] < row[None, :]
    n_named = jnp.sum(named)
    rank_named = jnp.sum((before & named[:, None]).astype(jnp.int32), axis=0)
    slot = jnp.where(named, rank_named, n_named + row - rank_named)
    return row[:, None] == slot[None, :]


def body(
    queries,
    key_cache,
    value_cache,
    lengths,
    out_proj,
    residual,
    routes,
    route_weight,
    w_gate,
    w_up,
    w_down,
):
    place = jnp.stack([lax.axis_index(a) for a in ("xhi", "z", "core")]).astype(jnp.int32)
    o_oth = swap_cores(out_proj)

    order = slots(routes)
    order16 = order.astype(jnp.bfloat16)
    share = jnp.sum(jnp.where(routes == 0, route_weight, 0.0), axis=1)
    share = jnp.sum(jnp.where(order, share[None, :], 0.0), axis=1)

    res = jnp.dot(order16, residual, preferred_element_type=jnp.float32)
    attended = attend(queries, key_cache, value_cache, lengths)
    attended = jnp.dot(order16, attended, preferred_element_type=jnp.float32).astype(jnp.bfloat16)
    by_heads = lax.all_to_all(
        attended.reshape(ROWS, CHIPS, 2 * HS), RING, split_axis=1, concat_axis=0
    )
    by_heads, o_oth, w_gate, w_up, w_down = lax.optimization_barrier(
        (by_heads, o_oth, w_gate, w_up, w_down)
    )
    g_oth, u_oth, d_oth = swap_cores(w_gate), swap_cores(w_up), swap_cores(w_down)
    parts, near, far = project(place, by_heads, out_proj, o_oth)
    half = far.shape[0] // 2
    mine, first, second = sum_z(cut(parts), swap_x(far[:half]), swap_x(far[half:]))
    rest = add16(near, jnp.concatenate([first, second], axis=0))

    chosen = add(res[:CAP], mine[:CAP])
    mine = jnp.concatenate([chosen.astype(jnp.bfloat16), mine[CAP:]], axis=0)
    theirs = swap_x(mine)
    chosen = add(chosen, theirs[CAP:])
    pair = add(mine, jnp.concatenate([theirs[CAP:], theirs[:CAP]], axis=0))
    normed = (
        pair * lax.rsqrt(jnp.mean(pair * pair, axis=1, keepdims=True) + 1e-06)
    ).astype(jnp.bfloat16)
    pieces = gather_z(normed)
    rows = expert(pieces, (w_gate, g_oth, w_up, u_oth, w_down, d_oth))
    both = [jnp.concatenate(p, axis=0) for p in zip(cut(rows), cut(rest))]
    got, _, _ = sum_z(both)
    expert_rows = add(got[:CAP], swap_x(got[CAP : NX * CAP]))
    others = add(res[CAP:], got[NX * CAP :])
    done = jnp.concatenate(
        [chosen + share[:CAP, None] * expert_rows, others], axis=0
    ).astype(jnp.bfloat16)
    return jnp.dot(order16.T, done, preferred_element_type=jnp.float32).astype(jnp.bfloat16)


def solution(mesh):
    fine = Mesh(mesh.devices.reshape(4, 2, NX, NZ, 2), AXES)
    rows, weights = P(AXES, None), P(("xhi", "z", "core"), None)
    placed = (
        rows,
        P(AXES, None, None),
        P(AXES, None, None),
        P(AXES),
        weights,
        rows,
        rows,
        rows,
        weights,
        weights,
        weights,
    )
    return jax.shard_map(body, mesh=fine, in_specs=placed, out_specs=rows, check_vma=False)
```

```python
import functools
import math

import jax
import jax.numpy as jnp
from jax import lax
from jax.experimental import pallas as pl
from jax.experimental.pallas import tpu as pltpu
from jax.sharding import Mesh
from jax.sharding import PartitionSpec as P

D = 7168
HS = 256
CAP = 8
NX = 2
NZ = 8
CHIPS = NX * NZ
ROWS = 16
AXES = ("y", "xlo", "xhi", "z", "core")
RING = ("xhi", "z")


def attend(queries, key_cache, value_cache, lengths):
    count_rows = queries.shape[0]
    cache_len = key_cache.shape[1]
    head_size = key_cache.shape[2]
    num_heads = queries.shape[1] // head_size
    grouped = queries.reshape(count_rows, num_heads, head_size)
    scores = jnp.einsum(
        "rhd,rld->rhl", grouped, key_cache, preferred_element_type=jnp.float32
    ) / math.sqrt(head_size)
    positions = lax.broadcasted_iota(jnp.int32, scores.shape, 2)
    valid = jnp.broadcast_to(lengths[:, None, None], scores.shape)
    scores = jnp.where(positions < valid, scores, -1e30)
    largest = jnp.max(scores, axis=2, keepdims=True)
    expo = jnp.exp(scores - largest)
    weights = (expo / jnp.sum(expo, axis=2, keepdims=True)).astype(jnp.bfloat16)
    mixed = jnp.einsum("rhl,rld->rhd", weights, value_cache, preferred_element_type=jnp.float32)
    return mixed.astype(jnp.bfloat16).reshape(count_rows, num_heads * head_size)


def swap_cores(a):
    return lax.ppermute(a, "core", [(0, 1), (1, 0)])


def swap_x(a):
    return lax.ppermute(a, "xhi", [(0, 1), (1, 0)])


def shift(a, by):
    return lax.ppermute(a, "z", [(i, (i + by) % NZ) for i in range(NZ)])


def add(*terms):
    total = terms[0].astype(jnp.float32)
    for term in terms[1:]:
        total = total + term.astype(jnp.float32)
    return total


def add16(*terms):
    return add(*terms).astype(jnp.bfloat16)


def sum_z(part, early=None, late=None):
    half = part[0].shape[-1] // 2
    left, right = [p[:, :half] for p in part], [p[:, half:] for p in part]
    a, b = shift(left[4], 1), shift(right[4], -1)
    c, d = shift(right[3], 1), shift(left[5], -1)
    a, b = shift(add16(left[3], a), 1), shift(add16(right[5], b), -1)
    c, d = shift(add16(right[2], c), 1), shift(add16(left[6], d), -1)
    if early is None:
        a, b, c, d = lax.optimization_barrier((a, b, c, d))
    else:
        a, b, c, d, early = lax.optimization_barrier((a, b, c, d, early))
    a, b = shift(add16(left[2], a), 1), shift(add16(right[6], b), -1)
    c, d = shift(add16(right[1], c), 1), shift(add16(left[7], d), -1)
    a, b = shift(add16(left[1], a), 1), shift(add16(right[7], b), -1)
    if late is not None:
        a, b, c, d, late = lax.optimization_barrier((a, b, c, d, late))
    total = jnp.concatenate([add16(left[0], a, d), add16(right[0], b, c)], axis=1)
    return total, early, late


def cut(part):
    both = part.shape[0] // NZ
    return [part[k * both : (k + 1) * both] for k in range(NZ)]


def gather_z(mine):
    half = mine.shape[-1] // 2
    a1, b1 = shift(mine, 1), shift(mine, -1)
    a2, b2 = shift(a1, 1), shift(b1, -1)
    a3, b3 = shift(a2, 1), shift(b2, -1)
    a4, b4 = shift(a3[..., :half], 1), shift(b3[..., half:], -1)
    return [mine, b1, b2, b3, a4, b4, a3, a2, a1]


def project_kernel(tile, place, a, w_own, w_oth, out, near, far, held, sems):
    steps, depth = D // tile, w_own.shape[0]
    moves = [
        [
            pltpu.make_async_copy(w.at[:, pl.ds(i * tile, tile)], held.at[k, i], sems.at[k, i])
            for k, w in enumerate((w_own, w_oth))
        ]
        for i in range(steps)
    ]
    for move in moves:
        for copy in move:
            copy.start()
    pairs = [(rx, rz) for rx in range(NX) for rz in range(NZ)]
    blocks = []
    for kind, order in enumerate((sorted(pairs, key=lambda p: p[1]), pairs)):
        for rx, rz in order:
            x = lax.rem(place[0] + rx, NX)
            z = lax.rem(place[1] + rz, NZ)
            block = a[x * NZ + z].astype(jnp.float32)
            blocks.append(block[kind * CAP : (kind + 1) * CAP])
    rows = jnp.concatenate(blocks, axis=0)
    first = place[2] == 0
    own = jnp.where(first, rows[:, :depth], rows[:, depth:]).astype(jnp.bfloat16)
    oth = jnp.where(first, rows[:, depth:], rows[:, :depth]).astype(jnp.bfloat16)
    for i in range(steps):
        for copy in moves[i]:
            copy.wait()
        total = jnp.dot(own, held[0, i], preferred_element_type=jnp.float32)
        total += jnp.dot(oth, held[1, i], preferred_element_type=jnp.float32)
        total = total.astype(jnp.bfloat16)
        at = slice(i * tile, (i + 1) * tile)
        top, middle = out.shape[0], out.shape[0] + near.shape[0]
        out[:, at], near[:, at], far[:, at] = total[:top], total[top:middle], total[middle:]


def project(place, attended, w_own, w_oth, tile=1024):
    rows, depth = CHIPS * CAP, w_own.shape[0]
    whole = pl.BlockSpec(memory_space=pltpu.VMEM)
    anywhere = pl.BlockSpec(memory_space=pl.ANY)
    return pl.pallas_call(
        functools.partial(project_kernel, tile),
        out_shape=[
            jax.ShapeDtypeStruct((n, D), jnp.bfloat16) for n in (rows, rows // NX, rows // NX)
        ],
        in_specs=[pl.BlockSpec(memory_space=pltpu.SMEM), whole, anywhere, anywhere],
        out_specs=[whole] * 3,
        scratch_shapes=[
            pltpu.VMEM((2, D // tile, depth, tile), jnp.bfloat16),
            pltpu.SemaphoreType.DMA((2, D // tile)),
        ],
        compiler_params=pltpu.CompilerParams(vmem_limit_bytes=50 * 1024 * 1024),
        cost_estimate=pl.CostEstimate(
            flops=8 * rows * depth * D, bytes_accessed=6 * depth * D, transcendentals=0
        ),
        name="project",
    )(place, attended, w_own, w_oth)


def expert_kernel(tile, *refs):
    pieces, first, (d_own, d_oth, out) = refs[:9], refs[9:13], refs[13:]
    steps, units = D // tile, d_own.shape[0]
    dims = (((1,), (1,)), ((), ()))
    both = None
    for i in range(steps):
        lo, hi = i * tile, (i + 1) * tile
        if hi <= D // 2:
            far = pieces[4][:, lo:hi]
        else:
            far = pieces[5][:, lo - D // 2 : hi - D // 2]
        near = [p[:, lo:hi] for p in pieces[:4]]
        back = [p[:, lo:hi] for p in pieces[6:]]
        piece = jnp.concatenate(near + [far] + back, axis=0)
        weights = jnp.concatenate([w[:, lo:hi] for w in first], axis=0)
        term = lax.dot_general(piece, weights, dims, preferred_element_type=jnp.float32)
        both = term if both is None else both + term
    gate, up = both[:, : 2 * units], both[:, 2 * units :]
    act = (gate / (1.0 + jnp.exp(-gate)) * up).astype(jnp.bfloat16)
    for i in range(steps):
        at = slice(i * tile, (i + 1) * tile)
        last = jnp.concatenate([d_own[:, at], d_oth[:, at]], axis=0)
        out[:, at] = jnp.dot(act, last, preferred_element_type=jnp.float32).astype(jnp.bfloat16)


def expert(pieces, weights, tile=896):
    whole = pl.BlockSpec(memory_space=pltpu.VMEM)
    return pl.pallas_call(
        functools.partial(expert_kernel, tile),
        out_shape=jax.ShapeDtypeStruct((CHIPS * CAP, D), jnp.bfloat16),
        in_specs=[whole] * (len(pieces) + len(weights)),
        out_specs=whole,
        compiler_params=pltpu.CompilerParams(vmem_limit_bytes=16 * 1024 * 1024),
        name="expert",
    )(*pieces, *weights)


def slots(routes):
    row = jnp.arange(ROWS)
    rank = jnp.where(jnp.any(routes == 0, axis=1), row, row + ROWS)
    slot = jnp.sum((rank[:, None] < rank[None, :]).astype(jnp.int32), axis=0)
    return row[:, None] == slot[None, :]


def body(
    queries,
    key_cache,
    value_cache,
    lengths,
    out_proj,
    residual,
    routes,
    route_weight,
    w_gate,
    w_up,
    w_down,
):
    place = jnp.stack([lax.axis_index(a) for a in ("xhi", "z", "core")]).astype(jnp.int32)
    o_oth = swap_cores(out_proj)

    order = slots(routes)
    order16 = order.astype(jnp.bfloat16)
    share = jnp.sum(jnp.where(routes == 0, route_weight, 0.0), axis=1)
    share = jnp.sum(jnp.where(order, share[None, :], 0.0), axis=1)

    res = jnp.dot(order16, residual, preferred_element_type=jnp.float32)
    attended = attend(queries, key_cache, value_cache, lengths)
    attended = jnp.dot(order16, attended, preferred_element_type=jnp.float32).astype(jnp.bfloat16)
    by_heads = lax.all_to_all(
        attended.reshape(ROWS, CHIPS, 2 * HS), RING, split_axis=1, concat_axis=0
    )
    by_heads, o_oth, w_gate, w_up, w_down = lax.optimization_barrier(
        (by_heads, o_oth, w_gate, w_up, w_down)
    )
    g_oth, u_oth, d_oth = swap_cores(w_gate), swap_cores(w_up), swap_cores(w_down)
    parts, near, far = project(place, by_heads, out_proj, o_oth)
    half = far.shape[0] // 2
    mine, first, second = sum_z(cut(parts), swap_x(far[:half]), swap_x(far[half:]))
    rest = add16(near, jnp.concatenate([first, second], axis=0))

    chosen = add(res[:CAP], mine[:CAP])
    mine = jnp.concatenate([chosen.astype(jnp.bfloat16), mine[CAP:]], axis=0)
    theirs = swap_x(mine)
    chosen = add(chosen, theirs[CAP:])
    pair = add(mine, jnp.concatenate([theirs[CAP:], theirs[:CAP]], axis=0))
    normed = (
        pair * lax.rsqrt(jnp.mean(pair * pair, axis=1, keepdims=True) + 1e-06)
    ).astype(jnp.bfloat16)
    pieces = gather_z(normed)
    rows = expert(pieces, (w_gate, g_oth, w_up, u_oth, w_down, d_oth))
    both = [jnp.concatenate(p, axis=0) for p in zip(cut(rows), cut(rest))]
    got, _, _ = sum_z(both)
    expert_rows = add(got[:CAP], swap_x(got[CAP : NX * CAP]))
    others = add(res[CAP:], got[NX * CAP :])
    done = jnp.concatenate(
        [chosen + share[:CAP, None] * expert_rows, others], axis=0
    ).astype(jnp.bfloat16)
    return jnp.dot(order16.T, done, preferred_element_type=jnp.float32).astype(jnp.bfloat16)


def solution(mesh):
    fine = Mesh(mesh.devices.reshape(4, 2, NX, NZ, 2), AXES)
    rows, weights = P(AXES, None), P(("xhi", "z", "core"), None)
    placed = (
        rows,
        P(AXES, None, None),
        P(AXES, None, None),
        P(AXES),
        weights,
        rows,
        rows,
        rows,
        weights,
        weights,
        weights,
    )
    return jax.shard_map(body, mesh=fine, in_specs=placed, out_specs=rows, check_vma=False)
```

```python
import functools
import math

import jax
import jax.numpy as jnp
from jax import lax
from jax.experimental import pallas as pl
from jax.experimental.pallas import tpu as pltpu
from jax.sharding import Mesh
from jax.sharding import PartitionSpec as P

D = 7168
HS = 256
CAP = 8
NX = 2
NZ = 8
CHIPS = NX * NZ
ROWS = 16
AXES = ("y", "xlo", "xhi", "z", "core")
RING = ("xhi", "z")


def attend(queries, key_cache, value_cache, lengths):
    count_rows = queries.shape[0]
    cache_len = key_cache.shape[1]
    head_size = key_cache.shape[2]
    num_heads = queries.shape[1] // head_size
    grouped = queries.reshape(count_rows, num_heads, head_size)
    scores = jnp.einsum(
        "rhd,rld->rhl", grouped, key_cache, preferred_element_type=jnp.float32
    ) / math.sqrt(head_size)
    positions = lax.broadcasted_iota(jnp.int32, scores.shape, 2)
    valid = jnp.broadcast_to(lengths[:, None, None], scores.shape)
    scores = jnp.where(positions < valid, scores, -1e30)
    largest = jnp.max(scores, axis=2, keepdims=True)
    expo = jnp.exp(scores - largest)
    weights = (expo / jnp.sum(expo, axis=2, keepdims=True)).astype(jnp.bfloat16)
    mixed = jnp.einsum("rhl,rld->rhd", weights, value_cache, preferred_element_type=jnp.float32)
    return mixed.astype(jnp.bfloat16).reshape(count_rows, num_heads * head_size)


def swap_cores(a):
    return lax.ppermute(a, "core", [(0, 1), (1, 0)])


def swap_x(a):
    return lax.ppermute(a, "xhi", [(0, 1), (1, 0)])


def shift(a, by):
    return lax.ppermute(a, "z", [(i, (i + by) % NZ) for i in range(NZ)])


def add(*terms):
    total = terms[0].astype(jnp.float32)
    for term in terms[1:]:
        total = total + term.astype(jnp.float32)
    return total


def add16(*terms):
    return add(*terms).astype(jnp.bfloat16)


def sum_z(part, early=None, late=None):
    half = part[0].shape[-1] // 2
    left, right = [p[:, :half] for p in part], [p[:, half:] for p in part]
    a, b = shift(left[4], 1), shift(right[4], -1)
    c, d = shift(right[3], 1), shift(left[5], -1)
    a, b = shift(add16(left[3], a), 1), shift(add16(right[5], b), -1)
    c, d = shift(add16(right[2], c), 1), shift(add16(left[6], d), -1)
    if early is None:
        a, b, c, d = lax.optimization_barrier((a, b, c, d))
    else:
        a, b, c, d, early = lax.optimization_barrier((a, b, c, d, early))
    a, b = shift(add16(left[2], a), 1), shift(add16(right[6], b), -1)
    c, d = shift(add16(right[1], c), 1), shift(add16(left[7], d), -1)
    a, b = shift(add16(left[1], a), 1), shift(add16(right[7], b), -1)
    if late is not None:
        a, b, c, d, late = lax.optimization_barrier((a, b, c, d, late))
    total = jnp.concatenate([add16(left[0], a, d), add16(right[0], b, c)], axis=1)
    return total, early, late


def cut(part):
    both = part.shape[0] // NZ
    return [part[k * both : (k + 1) * both] for k in range(NZ)]


def gather_z(mine):
    half = mine.shape[-1] // 2
    left, right = mine[:, :half], mine[:, half:]
    a, b, c, d = [left], [right], [right], [left]
    for step in range(4):
        a.append(shift(a[-1], 1))
        b.append(shift(b[-1], -1))
        if step < 3:
            c.append(shift(c[-1], 1))
            d.append(shift(d[-1], -1))
    return d + a[:0:-1] + b + c[:0:-1]


def project_kernel(tile, place, a, w_own, w_oth, out, near, far, held, sems):
    steps, depth = D // tile, w_own.shape[0]
    moves = [
        [
            pltpu.make_async_copy(w.at[:, pl.ds(i * tile, tile)], held.at[k, i], sems.at[k, i])
            for k, w in enumerate((w_own, w_oth))
        ]
        for i in range(steps)
    ]
    for move in moves:
        for copy in move:
            copy.start()
    pairs = [(rx, rz) for rx in range(NX) for rz in range(NZ)]
    blocks = []
    for kind, order in enumerate((sorted(pairs, key=lambda p: p[1]), pairs)):
        for rx, rz in order:
            x = lax.rem(place[0] + rx, NX)
            z = lax.rem(place[1] + rz, NZ)
            block = a[x * NZ + z].astype(jnp.float32)
            blocks.append(block[kind * CAP : (kind + 1) * CAP])
    rows = jnp.concatenate(blocks, axis=0)
    first = place[2] == 0
    own = jnp.where(first, rows[:, :depth], rows[:, depth:]).astype(jnp.bfloat16)
    oth = jnp.where(first, rows[:, depth:], rows[:, :depth]).astype(jnp.bfloat16)
    for i in range(steps):
        for copy in moves[i]:
            copy.wait()
        total = jnp.dot(own, held[0, i], preferred_element_type=jnp.float32)
        total += jnp.dot(oth, held[1, i], preferred_element_type=jnp.float32)
        total = total.astype(jnp.bfloat16)
        at = slice(i * tile, (i + 1) * tile)
        top, middle = out.shape[0], out.shape[0] + near.shape[0]
        out[:, at], near[:, at], far[:, at] = total[:top], total[top:middle], total[middle:]


def project(place, attended, w_own, w_oth, tile=1024):
    rows, depth = CHIPS * CAP, w_own.shape[0]
    whole = pl.BlockSpec(memory_space=pltpu.VMEM)
    anywhere = pl.BlockSpec(memory_space=pl.ANY)
    return pl.pallas_call(
        functools.partial(project_kernel, tile),
        out_shape=[
            jax.ShapeDtypeStruct((n, D), jnp.bfloat16) for n in (rows, rows // NX, rows // NX)
        ],
        in_specs=[pl.BlockSpec(memory_space=pltpu.SMEM), whole, anywhere, anywhere],
        out_specs=[whole] * 3,
        scratch_shapes=[
            pltpu.VMEM((2, D // tile, depth, tile), jnp.bfloat16),
            pltpu.SemaphoreType.DMA((2, D // tile)),
        ],
        compiler_params=pltpu.CompilerParams(vmem_limit_bytes=50 * 1024 * 1024),
        cost_estimate=pl.CostEstimate(
            flops=8 * rows * depth * D, bytes_accessed=6 * depth * D, transcendentals=0
        ),
        name="project",
    )(place, attended, w_own, w_oth)


def expert_kernel(tile, *refs):
    left, right = refs[:NZ], refs[NZ : 2 * NZ]
    first, (d_own, d_oth, out) = refs[2 * NZ : 2 * NZ + 4], refs[2 * NZ + 4 :]
    steps, units = D // tile, d_own.shape[0]
    dims = (((1,), (1,)), ((), ()))
    both = None
    for i in range(steps):
        lo, hi = i * tile, (i + 1) * tile
        side, at = (left, lo) if hi <= D // 2 else (right, lo - D // 2)
        piece = jnp.concatenate([p[:, at : at + tile] for p in side], axis=0)
        weights = jnp.concatenate([w[:, lo:hi] for w in first], axis=0)
        term = lax.dot_general(piece, weights, dims, preferred_element_type=jnp.float32)
        both = term if both is None else both + term
    gate, up = both[:, : 2 * units], both[:, 2 * units :]
    act = (gate / (1.0 + jnp.exp(-gate)) * up).astype(jnp.bfloat16)
    for i in range(steps):
        at = slice(i * tile, (i + 1) * tile)
        last = jnp.concatenate([d_own[:, at], d_oth[:, at]], axis=0)
        out[:, at] = jnp.dot(act, last, preferred_element_type=jnp.float32).astype(jnp.bfloat16)


def expert(pieces, weights, tile=896):
    whole = pl.BlockSpec(memory_space=pltpu.VMEM)
    return pl.pallas_call(
        functools.partial(expert_kernel, tile),
        out_shape=jax.ShapeDtypeStruct((CHIPS * CAP, D), jnp.bfloat16),
        in_specs=[whole] * (len(pieces) + len(weights)),
        out_specs=whole,
        compiler_params=pltpu.CompilerParams(vmem_limit_bytes=16 * 1024 * 1024),
        name="expert",
    )(*pieces, *weights)


def slots(routes):
    row = jnp.arange(ROWS)
    rank = jnp.where(jnp.any(routes == 0, axis=1), row, row + ROWS)
    slot = jnp.sum((rank[:, None] < rank[None, :]).astype(jnp.int32), axis=0)
    return row[:, None] == slot[None, :]


def body(
    queries,
    key_cache,
    value_cache,
    lengths,
    out_proj,
    residual,
    routes,
    route_weight,
    w_gate,
    w_up,
    w_down,
):
    place = jnp.stack([lax.axis_index(a) for a in ("xhi", "z", "core")]).astype(jnp.int32)
    o_oth = swap_cores(out_proj)

    order = slots(routes)
    order16 = order.astype(jnp.bfloat16)
    share = jnp.sum(jnp.where(routes == 0, route_weight, 0.0), axis=1)
    share = jnp.sum(jnp.where(order, share[None, :], 0.0), axis=1)

    res = jnp.dot(order16, residual, preferred_element_type=jnp.float32)
    attended = attend(queries, key_cache, value_cache, lengths)
    attended = jnp.dot(order16, attended, preferred_element_type=jnp.float32).astype(jnp.bfloat16)
    by_heads = lax.all_to_all(
        attended.reshape(ROWS, CHIPS, 2 * HS), RING, split_axis=1, concat_axis=0
    )
    by_heads, o_oth, w_gate, w_up, w_down = lax.optimization_barrier(
        (by_heads, o_oth, w_gate, w_up, w_down)
    )
    g_oth, u_oth, d_oth = swap_cores(w_gate), swap_cores(w_up), swap_cores(w_down)
    parts, near, far = project(place, by_heads, out_proj, o_oth)
    half = far.shape[0] // 2
    mine, first, second = sum_z(cut(parts), swap_x(far[:half]), swap_x(far[half:]))
    rest = add16(near, jnp.concatenate([first, second], axis=0))

    chosen = add(res[:CAP], mine[:CAP])
    mine = jnp.concatenate([chosen.astype(jnp.bfloat16), mine[CAP:]], axis=0)
    theirs = swap_x(mine)
    chosen = add(chosen, theirs[CAP:])
    pair = add(mine, jnp.concatenate([theirs[CAP:], theirs[:CAP]], axis=0))
    normed = (
        pair * lax.rsqrt(jnp.mean(pair * pair, axis=1, keepdims=True) + 1e-06)
    ).astype(jnp.bfloat16)
    pieces = gather_z(normed)
    rows = expert(pieces, (w_gate, g_oth, w_up, u_oth, w_down, d_oth))
    both = [jnp.concatenate(p, axis=0) for p in zip(cut(rows), cut(rest))]
    got, _, _ = sum_z(both)
    expert_rows = add(got[:CAP], swap_x(got[CAP : NX * CAP]))
    others = add(res[CAP:], got[NX * CAP :])
    done = jnp.concatenate(
        [chosen + share[:CAP, None] * expert_rows, others], axis=0
    ).astype(jnp.bfloat16)
    return jnp.dot(order16.T, done, preferred_element_type=jnp.float32).astype(jnp.bfloat16)


def solution(mesh):
    fine = Mesh(mesh.devices.reshape(4, 2, NX, NZ, 2), AXES)
    rows, weights = P(AXES, None), P(("xhi", "z", "core"), None)
    placed = (
        rows,
        P(AXES, None, None),
        P(AXES, None, None),
        P(AXES),
        weights,
        rows,
        rows,
        rows,
        weights,
        weights,
        weights,
    )
    return jax.shard_map(body, mesh=fine, in_specs=placed, out_specs=rows, check_vma=False)
```

```python
import functools
import math

import jax
import jax.numpy as jnp
from jax import lax
from jax.experimental import pallas as pl
from jax.experimental.pallas import tpu as pltpu
from jax.sharding import Mesh
from jax.sharding import PartitionSpec as P

D = 7168
HS = 256
CAP = 8
NX = 2
NZ = 8
CHIPS = NX * NZ
ROWS = 16
AXES = ("y", "xlo", "xhi", "z", "core")
RING = ("xhi", "z")


def attend(queries, key_cache, value_cache, lengths):
    count_rows = queries.shape[0]
    cache_len = key_cache.shape[1]
    head_size = key_cache.shape[2]
    num_heads = queries.shape[1] // head_size
    grouped = queries.reshape(count_rows, num_heads, head_size)
    scores = jnp.einsum(
        "rhd,rld->rhl", grouped, key_cache, preferred_element_type=jnp.float32
    ) / math.sqrt(head_size)
    positions = lax.broadcasted_iota(jnp.int32, scores.shape, 2)
    valid = jnp.broadcast_to(lengths[:, None, None], scores.shape)
    scores = jnp.where(positions < valid, scores, -1e30)
    largest = jnp.max(scores, axis=2, keepdims=True)
    expo = jnp.exp(scores - largest)
    weights = (expo / jnp.sum(expo, axis=2, keepdims=True)).astype(jnp.bfloat16)
    mixed = jnp.einsum("rhl,rld->rhd", weights, value_cache, preferred_element_type=jnp.float32)
    return mixed.astype(jnp.bfloat16).reshape(count_rows, num_heads * head_size)


def swap_cores(a):
    return lax.ppermute(a, "core", [(0, 1), (1, 0)])


def swap_x(a):
    return lax.ppermute(a, "xhi", [(0, 1), (1, 0)])


def shift(a, by):
    return lax.ppermute(a, "z", [(i, (i + by) % NZ) for i in range(NZ)])


def add(*terms):
    total = terms[0].astype(jnp.float32)
    for term in terms[1:]:
        total = total + term.astype(jnp.float32)
    return total


def add16(*terms):
    return add(*terms).astype(jnp.bfloat16)


def sum_z(part, early=None, late=None):
    half = part[0].shape[-1] // 2
    up, down = shift(part[4][:, :half], 1), shift(part[4][:, half:], -1)
    up = shift(add_part(part[3], up, 0), 1)
    down = shift(add_part(part[5], down, half), -1)
    if early is not None:
        up, down, early = lax.optimization_barrier((up, down, early))
    up = shift(add16(part[2], up), 1)
    down = shift(add16(part[6], down), -1)
    up = shift(add16(part[1], up), 1)
    down = shift(add16(part[7], down), -1)
    if late is not None:
        up, down, late = lax.optimization_barrier((up, down, late))
    return add16(part[0], up, down), early, late


def add_part(whole, piece, at):
    size = piece.shape[-1]
    added = add16(whole[:, at : at + size], piece)
    return jnp.concatenate([whole[:, :at], added, whole[:, at + size :]], axis=1)


def sum_z_four(part):
    half = part[0].shape[-1] // 2
    left, right = [p[:, :half] for p in part], [p[:, half:] for p in part]
    a, b = shift(left[4], 1), shift(right[4], -1)
    c, d = shift(right[3], 1), shift(left[5], -1)
    a, b = shift(add16(left[3], a), 1), shift(add16(right[5], b), -1)
    c, d = shift(add16(right[2], c), 1), shift(add16(left[6], d), -1)
    a, b, c, d = lax.optimization_barrier((a, b, c, d))
    a, b = shift(add16(left[2], a), 1), shift(add16(right[6], b), -1)
    c, d = shift(add16(right[1], c), 1), shift(add16(left[7], d), -1)
    a, b = shift(add16(left[1], a), 1), shift(add16(right[7], b), -1)
    return jnp.concatenate([add16(left[0], a, d), add16(right[0], b, c)], axis=1)


def cut(part):
    both = part.shape[0] // NZ
    return [part[k * both : (k + 1) * both] for k in range(NZ)]


def gather_z(mine):
    half = mine.shape[-1] // 2
    a1, b1 = shift(mine, 1), shift(mine, -1)
    a2, b2 = shift(a1, 1), shift(b1, -1)
    a3, b3 = shift(a2, 1), shift(b2, -1)
    a4, b4 = shift(a3[..., :half], 1), shift(b3[..., half:], -1)
    return [mine, b1, b2, b3, a4, b4, a3, a2, a1]


def project_kernel(tile, place, a, w_own, w_oth, out, near, far, held, sems):
    steps, depth = D // tile, w_own.shape[0]
    moves = [
        [
            pltpu.make_async_copy(w.at[:, pl.ds(i * tile, tile)], held.at[k, i], sems.at[k, i])
            for k, w in enumerate((w_own, w_oth))
        ]
        for i in range(steps)
    ]
    for move in moves:
        for copy in move:
            copy.start()
    pairs = [(rx, rz) for rx in range(NX) for rz in range(NZ)]
    blocks = []
    for kind, order in enumerate((sorted(pairs, key=lambda p: p[1]), pairs)):
        for rx, rz in order:
            x = lax.rem(place[0] + rx, NX)
            z = lax.rem(place[1] + rz, NZ)
            block = a[x * NZ + z].astype(jnp.float32)
            blocks.append(block[kind * CAP : (kind + 1) * CAP])
    rows = jnp.concatenate(blocks, axis=0)
    first = place[2] == 0
    own = jnp.where(first, rows[:, :depth], rows[:, depth:]).astype(jnp.bfloat16)
    oth = jnp.where(first, rows[:, depth:], rows[:, :depth]).astype(jnp.bfloat16)
    for i in range(steps):
        for copy in moves[i]:
            copy.wait()
        total = jnp.dot(own, held[0, i], preferred_element_type=jnp.float32)
        total += jnp.dot(oth, held[1, i], preferred_element_type=jnp.float32)
        total = total.astype(jnp.bfloat16)
        at = slice(i * tile, (i + 1) * tile)
        top, middle = out.shape[0], out.shape[0] + near.shape[0]
        out[:, at], near[:, at], far[:, at] = total[:top], total[top:middle], total[middle:]


def project(place, attended, w_own, w_oth, tile=1024):
    rows, depth = CHIPS * CAP, w_own.shape[0]
    whole = pl.BlockSpec(memory_space=pltpu.VMEM)
    anywhere = pl.BlockSpec(memory_space=pl.ANY)
    return pl.pallas_call(
        functools.partial(project_kernel, tile),
        out_shape=[
            jax.ShapeDtypeStruct((n, D), jnp.bfloat16) for n in (rows, rows // NX, rows // NX)
        ],
        in_specs=[pl.BlockSpec(memory_space=pltpu.SMEM), whole, anywhere, anywhere],
        out_specs=[whole] * 3,
        scratch_shapes=[
            pltpu.VMEM((2, D // tile, depth, tile), jnp.bfloat16),
            pltpu.SemaphoreType.DMA((2, D // tile)),
        ],
        compiler_params=pltpu.CompilerParams(vmem_limit_bytes=50 * 1024 * 1024),
        cost_estimate=pl.CostEstimate(
            flops=8 * rows * depth * D, bytes_accessed=6 * depth * D, transcendentals=0
        ),
        name="project",
    )(place, attended, w_own, w_oth)


def expert_kernel(tile, *refs):
    pieces, first, (d_own, d_oth, out) = refs[:9], refs[9:13], refs[13:]
    steps, units = D // tile, d_own.shape[0]
    dims = (((1,), (1,)), ((), ()))
    both = None
    for i in range(steps):
        lo, hi = i * tile, (i + 1) * tile
        if hi <= D // 2:
            far = pieces[4][:, lo:hi]
        else:
            far = pieces[5][:, lo - D // 2 : hi - D // 2]
        near = [p[:, lo:hi] for p in pieces[:4]]
        back = [p[:, lo:hi] for p in pieces[6:]]
        piece = jnp.concatenate(near + [far] + back, axis=0)
        weights = jnp.concatenate([w[:, lo:hi] for w in first], axis=0)
        term = lax.dot_general(piece, weights, dims, preferred_element_type=jnp.float32)
        both = term if both is None else both + term
    gate, up = both[:, : 2 * units], both[:, 2 * units :]
    act = (gate / (1.0 + jnp.exp(-gate)) * up).astype(jnp.bfloat16)
    for i in range(steps):
        at = slice(i * tile, (i + 1) * tile)
        last = jnp.concatenate([d_own[:, at], d_oth[:, at]], axis=0)
        out[:, at] = jnp.dot(act, last, preferred_element_type=jnp.float32).astype(jnp.bfloat16)


def expert(pieces, weights, tile=896):
    whole = pl.BlockSpec(memory_space=pltpu.VMEM)
    return pl.pallas_call(
        functools.partial(expert_kernel, tile),
        out_shape=jax.ShapeDtypeStruct((CHIPS * CAP, D), jnp.bfloat16),
        in_specs=[whole] * (len(pieces) + len(weights)),
        out_specs=whole,
        compiler_params=pltpu.CompilerParams(vmem_limit_bytes=16 * 1024 * 1024),
        name="expert",
    )(*pieces, *weights)


def slots(routes):
    row = jnp.arange(ROWS)
    rank = jnp.where(jnp.any(routes == 0, axis=1), row, row + ROWS)
    slot = jnp.sum((rank[:, None] < rank[None, :]).astype(jnp.int32), axis=0)
    return row[:, None] == slot[None, :]


def body(
    queries,
    key_cache,
    value_cache,
    lengths,
    out_proj,
    residual,
    routes,
    route_weight,
    w_gate,
    w_up,
    w_down,
):
    place = jnp.stack([lax.axis_index(a) for a in ("xhi", "z", "core")]).astype(jnp.int32)
    o_oth = swap_cores(out_proj)

    order = slots(routes)
    order16 = order.astype(jnp.bfloat16)
    share = jnp.sum(jnp.where(routes == 0, route_weight, 0.0), axis=1)
    share = jnp.sum(jnp.where(order, share[None, :], 0.0), axis=1)

    res = jnp.dot(order16, residual, preferred_element_type=jnp.float32)
    attended = attend(queries, key_cache, value_cache, lengths)
    attended = jnp.dot(order16, attended, preferred_element_type=jnp.float32).astype(jnp.bfloat16)
    by_heads = lax.all_to_all(
        attended.reshape(ROWS, CHIPS, 2 * HS), RING, split_axis=1, concat_axis=0
    )
    by_heads, o_oth, w_gate, w_up, w_down = lax.optimization_barrier(
        (by_heads, o_oth, w_gate, w_up, w_down)
    )
    g_oth, u_oth, d_oth = swap_cores(w_gate), swap_cores(w_up), swap_cores(w_down)
    parts, near, far = project(place, by_heads, out_proj, o_oth)
    half = far.shape[0] // 2
    mine, first, second = sum_z(cut(parts), swap_x(far[:half]), swap_x(far[half:]))
    rest = add16(near, jnp.concatenate([first, second], axis=0))

    chosen = add(res[:CAP], mine[:CAP])
    mine = jnp.concatenate([chosen.astype(jnp.bfloat16), mine[CAP:]], axis=0)
    theirs = swap_x(mine)
    chosen = add(chosen, theirs[CAP:])
    pair = add(mine, jnp.concatenate([theirs[CAP:], theirs[:CAP]], axis=0))
    normed = (
        pair * lax.rsqrt(jnp.mean(pair * pair, axis=1, keepdims=True) + 1e-06)
    ).astype(jnp.bfloat16)
    pieces = gather_z(normed)
    rows = expert(pieces, (w_gate, g_oth, w_up, u_oth, w_down, d_oth))
    both = [jnp.concatenate(p, axis=0) for p in zip(cut(rows), cut(rest))]
    got = sum_z_four(both)
    expert_rows = add(got[:CAP], swap_x(got[CAP : NX * CAP]))
    others = add(res[CAP:], got[NX * CAP :])
    done = jnp.concatenate(
        [chosen + share[:CAP, None] * expert_rows, others], axis=0
    ).astype(jnp.bfloat16)
    return jnp.dot(order16.T, done, preferred_element_type=jnp.float32).astype(jnp.bfloat16)


def solution(mesh):
    fine = Mesh(mesh.devices.reshape(4, 2, NX, NZ, 2), AXES)
    rows, weights = P(AXES, None), P(("xhi", "z", "core"), None)
    placed = (
        rows,
        P(AXES, None, None),
        P(AXES, None, None),
        P(AXES),
        weights,
        rows,
        rows,
        rows,
        weights,
        weights,
        weights,
    )
    return jax.shard_map(body, mesh=fine, in_specs=placed, out_specs=rows, check_vma=False)
```
